128 devices in a mesh: ctx: 16 (over x, y_lo, core), head: 8 (over y_hi, z).
Axes of the slice: x: 4, y: 4 (y_hi: 2, y_lo: 2; y = y_hi * 2 + y_lo), z: 4, core: 2. Of those that a mesh axis runs over, the one named last changes fastest.
Arguments:
- q_nope: bfloat16 [4096, 4096], P('ctx', 'head'), may hold values from -5 to 5
- q_rope: bfloat16 [4096, 2048], P('ctx', 'head'), may hold values from -320 to 320
- latent: bfloat16 [4096, 512], P('ctx'), may hold values from -5 to 5
- rope_keys: bfloat16 [4096, 64], P('ctx'), may hold values from -4.5 to 4.5
- out_grad: bfloat16 [4096, 4096], P('ctx', 'head'), may hold values from -96 to 96
- up_keys: bfloat16 [512, 4096], P(None, 'head'), may hold values from -0.25 to 0.25
- up_values: bfloat16 [512, 4096], P(None, 'head'), may hold values from -0.25 to 0.25
- group_order: int32 [32], replicated, may hold values from 0 to 31, each once
Outputs:
- grad_q_nope: bfloat16 [4096, 4096], P('ctx', 'head')
- grad_q_rope: bfloat16 [4096, 2048], P('ctx', 'head')
- grad_latent: float32 [4096, 512], P('ctx')
- grad_rope: float32 [4096, 64], P('ctx')
- grad_up_keys: float32 [512, 4096], P('ctx', 'head')
- grad_up_values: float32 [512, 4096], P('ctx', 'head')
The draws below stay inside these ranges and needn't reach their ends.
Inputs may be any that keep to these rules, and one draw needn't show every extreme that they name: `group_order`: each group place appears once.
All inputs are finite; a program needn't handle non-finite values.
Results may differ from the reference program's by a relative error of at most 0.0087.
Values may be sent and summed in bfloat16 or wider, within the bound.
A program may use at most 128 MiB of HBM per device.

```python
import jax
import jax.numpy as jnp
from jax import lax

LATENT = 512
ROPE = 64
HEAD_DIM = 128
HEADS = 32
SEQ = 4096
GROUP = 128
GROUPS = 32


def rope_base(key):
    return jnp.clip(jax.random.normal(jax.random.fold_in(key, 11), (SEQ, ROPE), jnp.float32), -4.0, 4.0)


def draw_rope_keys(key, part):
    base = rope_base(key)
    return base.astype(jnp.bfloat16)


def draw_q_rope(key, part):
    values = jnp.clip(jax.random.normal(jax.random.fold_in(key, 23), (SEQ, HEADS * ROPE), jnp.float32), -4.0, 4.0)
    return values.astype(jnp.bfloat16)


def steps_of(stream_key, extent, shards, smallest, top_value):
    gain = 1.0
    for axis_at, parts in shards:
        steps = jax.random.uniform(jax.random.fold_in(jax.random.fold_in(stream_key, 6), axis_at), (parts,), jnp.float32, smallest / len(shards), top_value / len(shards))
        gain = gain * jnp.repeat(jnp.exp(steps), extent[axis_at] // parts).reshape((-1,) + (1,) * (len(extent) - 1 - axis_at))
    return gain


def noise(key, dims, width, limit, split=(), held_as=jnp.bfloat16):
    level = steps_of(key, dims, split, -0.22, 0.18) if split else 1.0
    result = jax.random.normal(key, dims, jnp.float32) * width * level
    return jnp.minimum(jnp.maximum(result, -limit), limit).astype(held_as)


def setup_inputs(seed: int = 0) -> dict:
    splits = jax.random.split(jax.random.key(seed), 9)
    q_nope = noise(splits[0], (SEQ, HEADS * HEAD_DIM), 1.0, 5.0, ((0, 16), (1, 8)))
    q_rope = draw_q_rope(jax.random.fold_in(splits[8], 71), 0)
    latent = noise(splits[2], (SEQ, LATENT), 1.0, 5.0, ((0, 16),))
    rope_keys = draw_rope_keys(jax.random.fold_in(splits[8], 71), 0)
    out_grad = noise(splits[4], (SEQ, HEADS * HEAD_DIM), 16.0, 96.0, ((0, 16), (1, 8)))
    up_keys = noise(splits[5], (LATENT, HEADS * HEAD_DIM), LATENT ** -0.5, 0.25, ((1, 8),))
    up_values = noise(splits[6], (LATENT, HEADS * HEAD_DIM), LATENT ** -0.5, 0.25, ((1, 8),))
    group_order = jax.random.permutation(splits[7], GROUPS).astype(jnp.int32)
    return {"q_nope": q_nope, "q_rope": q_rope, "latent": latent, "rope_keys": rope_keys, "out_grad": out_grad, "up_keys": up_keys, "up_values": up_values, "group_order": group_order}


NEG_LARGE = -1e30


def reference(q_nope, q_rope, latent, rope_keys, out_grad, up_keys, up_values, group_order):
    seq_len = q_nope.shape[0]
    rows = jnp.arange(seq_len, dtype=jnp.int32)
    place = group_order[rows // GROUP] * GROUP + rows % GROUP
    visible = place[None, :] <= place[:, None]
    scale = (HEAD_DIM + ROPE) ** -0.5
    keys_all = jnp.dot(latent, up_keys, preferred_element_type=jnp.float32).astype(jnp.bfloat16)
    values_all = jnp.dot(latent, up_values, preferred_element_type=jnp.float32).astype(jnp.bfloat16)
    head_count = q_nope.shape[1] // HEAD_DIM

    def one_head(index):
        query_nope = lax.dynamic_slice_in_dim(q_nope, index * HEAD_DIM, HEAD_DIM, 1)
        query_rope = lax.dynamic_slice_in_dim(q_rope, index * ROPE, ROPE, 1)
        grad_head = lax.dynamic_slice_in_dim(out_grad, index * HEAD_DIM, HEAD_DIM, 1)
        key_rows = lax.dynamic_slice_in_dim(keys_all, index * HEAD_DIM, HEAD_DIM, 1)
        value_rows = lax.dynamic_slice_in_dim(values_all, index * HEAD_DIM, HEAD_DIM, 1)
        score = jnp.dot(query_nope, key_rows.T, preferred_element_type=jnp.float32)
        score = (score + jnp.dot(query_rope, rope_keys.T, preferred_element_type=jnp.float32)) * scale
        masked = jnp.where(visible, score, NEG_LARGE)
        row_top = jnp.max(masked, axis=1, keepdims=True)
        expd = jnp.where(visible, jnp.exp(masked - row_top), 0.0)
        attn = expd / jnp.sum(expd, axis=1, keepdims=True)
        dattn = jnp.dot(grad_head, value_rows.T, preferred_element_type=jnp.float32)
        delta = jnp.sum(attn * dattn, axis=1, keepdims=True)
        dscore = (attn * (dattn - delta)).astype(jnp.bfloat16)
        grad_nope = (jnp.dot(dscore, key_rows, preferred_element_type=jnp.float32) * scale).astype(jnp.bfloat16)
        grad_qrope = (jnp.dot(dscore, rope_keys, preferred_element_type=jnp.float32) * scale).astype(jnp.bfloat16)
        dkeys = (jnp.dot(dscore.T, query_nope, preferred_element_type=jnp.float32) * scale).astype(jnp.bfloat16)
        dvalues = jnp.dot(attn.astype(jnp.bfloat16).T, grad_head, preferred_element_type=jnp.float32).astype(jnp.bfloat16)
        drope = jnp.dot(dscore.T, query_rope, preferred_element_type=jnp.float32) * scale
        return grad_nope, grad_qrope, dkeys, dvalues, drope

    stacked = lax.map(one_head, jnp.arange(head_count, dtype=jnp.int32))

    def flatten(block):
        return jnp.transpose(block, (1, 0, 2)).reshape(seq_len, -1)

    grad_q_nope = flatten(stacked[0])
    grad_q_rope = flatten(stacked[1])
    dkeys_all = flatten(stacked[2])
    dvalues_all = flatten(stacked[3])
    grad_rope = jnp.sum(stacked[4], axis=0)
    grad_latent = jnp.dot(dkeys_all, up_keys.T, preferred_element_type=jnp.float32)
    grad_latent = grad_latent + jnp.dot(dvalues_all, up_values.T, preferred_element_type=jnp.float32)
    grad_up_keys = jnp.dot(latent.T, dkeys_all, preferred_element_type=jnp.float32)
    grad_up_values = jnp.dot(latent.T, dvalues_all, preferred_element_type=jnp.float32)
    return grad_q_nope, grad_q_rope, grad_latent, grad_rope, grad_up_keys, grad_up_values
```

```python
import functools
import math

import jax
import jax.numpy as jnp
from jax import lax
from jax.experimental import pallas as pl
from jax.experimental.pallas import tpu as pltpu
from jax.sharding import PartitionSpec as P

MESH = pl.DeviceIdType.MESH
F32 = jnp.float32
BF16 = jnp.bfloat16

SCALE = (128 + 64) ** (-0.5)
EXP2_SCALE = SCALE * math.log2(math.e)
NEG_LARGE = -1e30

GROUP = 128
GROUPS = 32
BLOCKS = 16
TOKENS = 256
ROWS = 640
DQ_ROWS = 384
CHUNK = 512
PAIR = 256
MIB = 1024 * 1024

NT = (((1,), (1,)), ((), ()))
TN = (((0,), (0,)), ((), ()))


def low_lanes(rows):
    return lax.broadcasted_iota(jnp.int32, (rows, 128), 1) < 64


def swap_halves(tile):
    return pltpu.roll(tile, 64, 1)


def place_of(me):
    x = lax.div(me, 4)
    quarter = lax.rem(me, 4)
    core = lax.rem(quarter, 2)
    y = lax.div(quarter, 2)
    y_mate = 4 * x + 2 * (1 - y) + core
    core_mate = 4 * x + 2 * y + (1 - core)
    return x, quarter, y, core, y_mate, core_mate


def remote(src, dst, send_sem, recv_sem, ctx):
    return pltpu.make_async_remote_copy(
        src_ref=src,
        dst_ref=dst,
        send_sem=send_sem,
        recv_sem=recv_sem,
        device_id={"ctx": ctx},
        device_id_type=MESH,
    )


def exchange_kernel(
    qn, qr, og, lat, rope, uk, uv, kv, qd,
    skv, sq, send_x, send_y, send_c, recv_kv, send_q, recv_q, local_sem,
):
    me = lax.axis_index("ctx")
    x, quarter, y, core, y_mate, core_mate = place_of(me)
    barrier = pltpu.get_barrier_semaphore()
    for o in (1, 2, 3):
        pl.semaphore_signal(
            barrier, inc=1, device_id={"ctx": 4 * lax.rem(x + o, 4) + quarter}, device_id_type=MESH
        )
    for mate in (y_mate, core_mate):
        pl.semaphore_signal(barrier, inc=1, device_id={"ctx": mate}, device_id_type=MESH)

    keys = jnp.dot(lat[...], uk[...], preferred_element_type=F32).astype(BF16)
    values = jnp.dot(lat[...], uv[...], preferred_element_type=F32).astype(BF16)
    rope_packed = jnp.concatenate([rope[0:128, :], rope[128:256, :]], axis=1)
    for h in range(4):
        skv[h, 0:256, :] = keys[:, 128 * h : 128 * h + 128]
        skv[h, 256:512, :] = values[:, 128 * h : 128 * h + 128]
        skv[h, 512:640, :] = rope_packed
    pl.semaphore_wait(barrier, 5)

    started = []
    for o in (1, 3, 2):
        other = lax.rem(x + o, 4)
        started.append(
            remote(skv.at[other], kv.at[me], send_x.at[o - 1], recv_kv.at[me], 4 * other + quarter)
        )
        started[-1].start()
    own = pltpu.make_async_copy(skv.at[x], kv.at[me], local_sem.at[0])
    own.start()
    started.append(remote(skv.at[x], kv.at[me], send_y.at[0], recv_kv.at[me], y_mate))
    started[-1].start()
    started.append(remote(skv.at[x], kv.at[me], send_c.at[0], recv_kv.at[me], core_mate))
    started[-1].start()

    low = low_lanes(128)
    for h in range(4):
        sq[h, 0:256, :] = qn[:, 128 * h : 128 * h + 128]
        sq[h, 256:512, :] = og[:, 128 * h : 128 * h + 128]
        tile = qr[:, 128 * (h // 2) : 128 * (h // 2) + 128].astype(F32)
        top, bottom = tile[0:128], tile[128:256]
        if h % 2 == 0:
            packed = jnp.where(low, top, swap_halves(bottom))
        else:
            packed = jnp.where(low, swap_halves(top), bottom)
        sq[h, 512:640, :] = packed.astype(BF16)
    for o in (1, 3, 2):
        other = lax.rem(x + o, 4)
        started.append(
            remote(sq.at[other], qd.at[x], send_q.at[o - 1], recv_q.at[x], 4 * other + quarter)
        )
        started[-1].start()
    own_q = pltpu.make_async_copy(sq.at[x], qd.at[x], local_sem.at[1])
    own_q.start()

    def arrived(block):
        remote(kv.at[block], kv.at[block], send_c.at[0], recv_kv.at[block], core_mate).wait_recv()

    for n, o in enumerate((1, 3, 2)):
        block = 4 * lax.rem(x + o, 4) + quarter
        arrived(block)
        started.append(
            remote(kv.at[block], kv.at[block], send_y.at[n + 1], recv_kv.at[block], y_mate)
        )
        started[-1].start()
        started.append(
            remote(kv.at[block], kv.at[block], send_c.at[n + 1], recv_kv.at[block], core_mate)
        )
        started[-1].start()
    for n, o in enumerate((0, 1, 3, 2)):
        block = 4 * lax.rem(x + o, 4) + 2 * (1 - y) + core
        arrived(block)
        started.append(
            remote(kv.at[block], kv.at[block], send_c.at[n + 4], recv_kv.at[block], core_mate)
        )
        started[-1].start()
    for o in range(4):
        for side in range(2):
            arrived(4 * o + 2 * side + (1 - core))
    for o in (1, 3, 2):
        other = lax.rem(x + o, 4)
        remote(sq.at[other], qd.at[other], send_q.at[0], recv_q.at[other], core_mate).wait_recv()
    own.wait()
    own_q.wait()
    for copy in started:
        copy.wait_send()


def exchange(qn, qr, og, lat, rope, uk, uv):
    vmem = pl.BlockSpec(memory_space=pltpu.VMEM)
    anywhere = pl.BlockSpec(memory_space=pl.ANY)
    return pl.pallas_call(
        exchange_kernel,
        name="exchange",
        out_shape=(
            jax.ShapeDtypeStruct((BLOCKS, ROWS, 128), BF16),
            jax.ShapeDtypeStruct((4, ROWS, 128), BF16),
        ),
        in_specs=[vmem] * 7,
        out_specs=(anywhere, anywhere),
        scratch_shapes=[
            pltpu.VMEM((4, ROWS, 128), BF16),
            pltpu.VMEM((4, ROWS, 128), BF16),
            pltpu.SemaphoreType.DMA((3,)),
            pltpu.SemaphoreType.DMA((4,)),
            pltpu.SemaphoreType.DMA((8,)),
            pltpu.SemaphoreType.DMA((BLOCKS,)),
            pltpu.SemaphoreType.DMA((3,)),
            pltpu.SemaphoreType.DMA((4,)),
            pltpu.SemaphoreType.DMA((2,)),
        ],
        compiler_params=pltpu.CompilerParams(
            collective_id=0, has_side_effects=True, vmem_limit_bytes=32 * MIB
        ),
    )(qn, qr, og, lat, rope, uk, uv)


def attention_kernel(
    order, kv, qd, dkv, dq,
    held, q_place, q_group, kc, kt, vc, rp, qc, qct, doc, doct, s_all, dp_all, dkc, dvc, dqt,
    dq_rope, dk_rope, sems,
):
    quarter = lax.rem(lax.axis_index("ctx"), 4)

    @pl.loop(0, GROUPS)
    def _(g):
        held[order[g]] = g

    def load_copies(p):
        g = held[p]
        block, row = lax.div(g, 2), pl.multiple_of(lax.rem(g, 2) * GROUP, GROUP)
        to = pl.ds(pl.multiple_of(p * GROUP, GROUP), GROUP)
        return (
            pltpu.make_async_copy(
                kv.at[block, pl.ds(row, GROUP), :], kc.at[to, pl.ds(0, 128)], sems.at[0, p]
            ),
            pltpu.make_async_copy(kv.at[block, pl.ds(256 + row, GROUP), :], vc.at[to, :], sems.at[1, p]),
            pltpu.make_async_copy(kv.at[block, pl.ds(512, GROUP), :], rp.at[to, :], sems.at[2, p]),
        )

    @pl.loop(0, GROUPS)
    def _(p):
        for copy in load_copies(p):
            copy.start()

    q_place[8] = 0

    @pl.loop(0, GROUPS, init_carry=jnp.int32(0))
    def _(p, n):
        g = held[p]
        mine = lax.rem(lax.div(g, 2), 4) == quarter
        q_place[n] = p
        q_group[n] = g
        return n + jnp.where(mine, 1, 0)

    low = low_lanes(GROUP)
    low_int = low.astype(jnp.int32)

    @pl.loop(0, 8)
    def _(n):
        g = q_group[n]
        slot, half = lax.div(g, 8), lax.rem(g, 2)
        row = pl.multiple_of(half * GROUP, GROUP)
        to = pl.ds(pl.multiple_of(n * GROUP, GROUP), GROUP)
        qc[to, 0:128] = qd[slot, pl.ds(row, GROUP), :]
        doc[to, :] = qd[slot, pl.ds(256 + row, GROUP), :]
        packed = qd[slot, 512:640, :].astype(F32)
        keep = low_int == 1 - half
        qc[to, 128:256] = jnp.where(keep, packed, swap_halves(packed)).astype(BF16)

    @pl.loop(0, GROUPS * GROUP // CHUNK)
    def _(c):
        rows = pl.ds(pl.multiple_of(c * CHUNK, CHUNK), CHUNK)
        dkc[rows, :] = jnp.zeros((CHUNK, 256), F32)
        dvc[rows, :] = jnp.zeros((CHUNK, 128), F32)

    for i in range(4):
        qct[i] = qc[PAIR * i : PAIR * i + PAIR, :].T
        doct[i] = doc[PAIR * i : PAIR * i + PAIR, :].T

    @pl.loop(0, GROUPS)
    def _(p):
        for copy in load_copies(p):
            copy.wait()
        half = lax.rem(held[p], 2)
        to = pl.ds(pl.multiple_of(p * GROUP, GROUP), GROUP)
        keep = low_int == 1 - half
        rope = jnp.where(keep, rp[to, :].astype(F32), 0.0).astype(BF16)
        kc[to, 128:256] = rope
        kt[p, 0:128, :] = kc[to, 0:128].T
        kt[p, 128:256, :] = rope.T

    row_iota = lax.broadcasted_iota(jnp.int32, (CHUNK, PAIR), 0)
    lane_iota = lax.broadcasted_iota(jnp.int32, (1, PAIR), 1)

    def by_eights(block):
        return block.reshape(CHUNK // 8, 8, PAIR)

    @pl.loop(0, 4)
    def _(i):
        place_a, place_b = q_place[2 * i], q_place[2 * i + 1]
        whole = lax.div(place_a, CHUNK // GROUP)
        count = lax.div(place_b, CHUNK // GROUP) + 1
        q_pos = jnp.where(
            lane_iota < GROUP, place_a * GROUP + lane_iota, (place_b - 1) * GROUP + lane_iota
        )
        q_rows = pl.ds(pl.multiple_of(i * PAIR, PAIR), PAIR)

        def scores(c, top, masked):
            rows = pl.ds(pl.multiple_of(c * CHUNK, CHUNK), CHUNK)
            s = jnp.dot(kc[rows, :], qct[i], preferred_element_type=F32)
            if masked:
                s = jnp.where(row_iota + c * CHUNK <= q_pos, s, NEG_LARGE)
            s_all[rows, :] = s
            dp_all[rows, :] = jnp.dot(vc[rows, :], doct[i], preferred_element_type=F32)
            return jnp.maximum(top, jnp.max(by_eights(s), axis=0))

        top = jnp.full((8, PAIR), NEG_LARGE, F32)
        top = lax.fori_loop(0, whole, lambda c, t: scores(c, t, False), top)
        top = lax.fori_loop(whole, count, lambda c, t: scores(c, t, True), top)
        top = jnp.max(top, axis=0, keepdims=True)

        def exps(c, carry):
            total, weighted = carry
            rows = pl.ds(pl.multiple_of(c * CHUNK, CHUNK), CHUNK)
            p = jnp.exp2((s_all[rows, :] - top) * EXP2_SCALE)
            s_all[rows, :] = p
            total = total + jnp.sum(by_eights(p), axis=0)
            weighted = weighted + jnp.sum(by_eights(p * dp_all[rows, :]), axis=0)
            return total, weighted

        zeros = jnp.zeros((8, PAIR), F32)
        total, weighted = lax.fori_loop(0, count, exps, (zeros, zeros))
        inverse = 1.0 / jnp.sum(total, axis=0, keepdims=True)
        delta = jnp.sum(weighted, axis=0, keepdims=True) * inverse
        dqt[...] = jnp.zeros((256, PAIR), F32)

        def grads(c, carry):
            rows = pl.ds(pl.multiple_of(c * CHUNK, CHUNK), CHUNK)
            attn = s_all[rows, :] * inverse
            ds = (attn * (dp_all[rows, :] - delta)).astype(BF16)
            dvc[rows, :] += jnp.dot(attn.astype(BF16), doc[q_rows, :], preferred_element_type=F32)
            dkc[rows, :] += jnp.dot(ds, qc[q_rows, :], preferred_element_type=F32)
            first = c * (CHUNK // GROUP)
            keys_t = jnp.concatenate([kt[first + n] for n in range(CHUNK // GROUP)], axis=1)
            dqt[...] += jnp.dot(keys_t, ds, preferred_element_type=F32)
            return carry

        lax.fori_loop(0, count, grads, 0)
        dq_pair = dqt[...].T * SCALE
        for n in range(2):
            g = q_group[2 * i + n]
            slot, half = lax.div(g, 8), lax.rem(g, 2)
            row = pl.multiple_of(half * GROUP, GROUP)
            part = dq_pair[GROUP * n : GROUP * n + GROUP]
            dq[slot, pl.ds(row, GROUP), :] = part[:, 0:128].astype(BF16)
            both = part[:, 128:256]
            dq_rope[2 * slot + half] = both + swap_halves(both)

    for slot in range(4):
        dq[slot, 256:384, :] = jnp.where(low, dq_rope[2 * slot], dq_rope[2 * slot + 1]).astype(BF16)

    @pl.loop(0, GROUPS)
    def _(p):
        g = held[p]
        block, row = lax.div(g, 2), pl.multiple_of(lax.rem(g, 2) * GROUP, GROUP)
        rows = pl.ds(pl.multiple_of(p * GROUP, GROUP), GROUP)
        dkv[block, pl.ds(row, GROUP), :] = (dkc[rows, 0:128] * SCALE).astype(BF16)
        dkv[block, pl.ds(256 + row, GROUP), :] = dvc[rows, :].astype(BF16)
        dk_rope[g] = dkc[rows, 128:256] * SCALE

    @pl.loop(0, BLOCKS)
    def _(block):
        dkv[block, 512:640, :] = jnp.where(low, dk_rope[2 * block], dk_rope[2 * block + 1]).astype(BF16)


def attention(order, kv, qd):
    vmem = pl.BlockSpec(memory_space=pltpu.VMEM)
    seq = GROUPS * GROUP
    return pl.pallas_call(
        attention_kernel,
        name="attention",
        out_shape=(
            jax.ShapeDtypeStruct((BLOCKS, ROWS, 128), BF16),
            jax.ShapeDtypeStruct((4, DQ_ROWS, 128), BF16),
        ),
        in_specs=[
            pl.BlockSpec(memory_space=pltpu.SMEM),
            pl.BlockSpec(memory_space=pl.ANY),
            vmem,
        ],
        out_specs=(vmem, vmem),
        scratch_shapes=[
            pltpu.SMEM((GROUPS,), jnp.int32),
            pltpu.SMEM((16,), jnp.int32),
            pltpu.SMEM((16,), jnp.int32),
            pltpu.VMEM((seq, 256), BF16),
            pltpu.VMEM((GROUPS, 256, GROUP), BF16),
            pltpu.VMEM((seq, 128), BF16),
            pltpu.VMEM((seq, 128), BF16),
            pltpu.VMEM((1024, 256), BF16),
            pltpu.VMEM((4, 256, PAIR), BF16),
            pltpu.VMEM((1024, 128), BF16),
            pltpu.VMEM((4, 128, PAIR), BF16),
            pltpu.VMEM((seq, PAIR), F32),
            pltpu.VMEM((seq, PAIR), F32),
            pltpu.VMEM((seq, 256), F32),
            pltpu.VMEM((seq, 128), F32),
            pltpu.VMEM((256, PAIR), F32),
            pltpu.VMEM((8, GROUP, 128), F32),
            pltpu.VMEM((GROUPS, GROUP, 128), F32),
            pltpu.SemaphoreType.DMA((3, GROUPS)),
        ],
        compiler_params=pltpu.CompilerParams(vmem_limit_bytes=48 * MIB),
    )(order, kv, qd)


def reduce_kernel(
    heads, dkv, dq, lat, uk, uv, gqn, gqr, gl, gr, guk, guv,
    rc, sy, ry, sx, rx, rdq, sl, rl, ag, gp, gc, sgy, rgy, sgx, rgx,
    send_c, recv_c, send_q, recv_q, send_y, recv_y, send_x, recv_x, send_l, recv_l, send_a, recv_a,
    send_g, recv_g, send_gx, recv_gx,
):
    me = lax.axis_index("ctx")
    head = lax.axis_index("head")
    x, quarter, y, core, y_mate, core_mate = place_of(me)
    piece = TOKENS // heads
    barrier = pltpu.get_barrier_semaphore()
    for o in (1, 2, 3):
        pl.semaphore_signal(
            barrier, inc=1, device_id={"ctx": 4 * lax.rem(x + o, 4) + quarter}, device_id_type=MESH
        )
    for mate in (y_mate, core_mate):
        pl.semaphore_signal(barrier, inc=1, device_id={"ctx": mate}, device_id_type=MESH)
    for o in range(1, heads):
        pl.semaphore_signal(
            barrier, inc=1, device_id={"head": lax.rem(head + o, heads)}, device_id_type=MESH
        )
    pl.semaphore_wait(barrier, 5 + heads - 1)

    started = []

    def send(*args):
        copy = remote(*args)
        copy.start()
        started.append(copy)

    turn = (1, 3, 2, 0)
    for far in (1, 0):
        for o in turn:
            other = lax.rem(x + o, 4)
            side = (1 - y) if far else y
            slot = 4 * (1 - far) + other
            send(
                dkv.at[4 * other + 2 * side + (1 - core)], rc.at[slot],
                send_c.at[slot], recv_c.at[slot], core_mate,
            )
    for o in (1, 3, 2):
        other = lax.rem(x + o, 4)
        send(dq.at[other], rdq.at[x], send_q.at[o - 1], recv_q.at[x], 4 * other + quarter)
    rdq[x] = dq[x]

    def from_core(slot):
        remote(rc.at[slot], rc.at[slot], send_c.at[0], recv_c.at[slot], core_mate).wait_recv()

    for o in turn:
        other = lax.rem(x + o, 4)
        from_core(other)
        sy[other] = (
            dkv[4 * other + 2 * (1 - y) + core].astype(F32) + rc[other].astype(F32)
        ).astype(BF16)
        send(sy.at[other], ry.at[other], send_y.at[other], recv_y.at[other], y_mate)
    for o in turn:
        other = lax.rem(x + o, 4)
        from_core(4 + other)
        near = dkv[4 * other + 2 * y + core].astype(F32) + rc[4 + other].astype(F32)
        remote(ry.at[other], ry.at[other], send_c.at[0], recv_y.at[other], y_mate).wait_recv()
        full = (near + ry[other].astype(F32)).astype(BF16)
        if o:
            sx[other] = full
            send(sx.at[other], rx.at[x], send_x.at[o - 1], recv_x.at[x], 4 * other + quarter)
        else:
            rx[x] = full

    low = low_lanes(128)
    for o in (1, 3, 2):
        other = lax.rem(x + o, 4)
        remote(rdq.at[other], rdq.at[other], send_c.at[0], recv_q.at[other], y_mate).wait_recv()
    for h in range(4):
        gqn[:, 128 * h : 128 * h + 128] = rdq[h, 0:256, :]
    for two in range(2):
        a = rdq[2 * two, 256:384, :].astype(F32)
        b = rdq[2 * two + 1, 256:384, :].astype(F32)
        cols = slice(128 * two, 128 * two + 128)
        gqr[0:128, cols] = jnp.where(low, a, swap_halves(b)).astype(BF16)
        gqr[128:256, cols] = jnp.where(low, swap_halves(a), b).astype(BF16)

    for o in (1, 3, 2):
        other = lax.rem(x + o, 4)
        remote(rx.at[other], rx.at[other], send_c.at[0], recv_x.at[other], y_mate).wait_recv()
    dkeys = jnp.concatenate([rx[h, 0:256, :] for h in range(4)], axis=1)
    dvalues = jnp.concatenate([rx[h, 256:512, :] for h in range(4)], axis=1)
    part = lax.dot_general(dkeys, uk[...], NT, preferred_element_type=F32)
    part = part + lax.dot_general(dvalues, uv[...], NT, preferred_element_type=F32)
    rope = rx[0, 512:640, :].astype(F32)
    for h in range(1, 4):
        rope = rope + rx[h, 512:640, :].astype(F32)
    half = piece // 2
    for p in range(heads):
        sl[p, :, 0:512] = part[piece * p : piece * p + piece].astype(BF16)
        sl[p, 0:half, 512:640] = rope[half * p : half * p + half].astype(BF16)
        sl[p, half:piece, 512:640] = jnp.zeros((piece - half, 128), BF16)

    def send_head(src, dst, send_sem, recv_sem, to):
        copy = pltpu.make_async_remote_copy(
            src_ref=src,
            dst_ref=dst,
            send_sem=send_sem,
            recv_sem=recv_sem,
            device_id={"head": to},
            device_id_type=MESH,
        )
        copy.start()
        started.append(copy)

    for o in range(1, heads):
        to = lax.rem(head + o, heads)
        send_head(sl.at[to], rl.at[head], send_l.at[o], recv_l.at[head], to)
    rl[head] = sl[head]

    weight_keys = lax.dot_general(lat[...], dkeys, TN, preferred_element_type=F32).astype(BF16)
    weight_values = lax.dot_general(lat[...], dvalues, TN, preferred_element_type=F32).astype(BF16)
    for cc in range(2):
        for yy in range(2):
            for xx in range(4):
                row = 32 * (4 * xx + 2 * yy + cc)
                gp[cc, yy, xx, :, 0:512] = weight_keys[row : row + 32]
                gp[cc, yy, xx, :, 512:1024] = weight_values[row : row + 32]
    send(gp.at[1 - core], gc, send_g.at[0], recv_g.at[0], core_mate)

    for o in range(1, heads):
        source = lax.rem(head + o, heads)
        remote(rl.at[source], rl.at[source], send_c.at[0], recv_l.at[source], y_mate).wait_recv()
    summed = rl[0].astype(F32)
    for p in range(1, heads):
        summed = summed + rl[p].astype(F32)
    ag[head] = summed.astype(BF16)
    for o in range(1, heads):
        to = lax.rem(head + o, heads)
        send_head(ag.at[head], ag.at[head], send_a.at[o], recv_a.at[head], to)

    remote(gc, gc, send_c.at[0], recv_g.at[0], core_mate).wait_recv()
    sgy[...] = (gp[core, 1 - y].astype(F32) + gc[1 - y].astype(F32)).astype(BF16)
    send(sgy, rgy, send_g.at[1], recv_g.at[1], y_mate)
    near_g = gp[core, y].astype(F32) + gc[y].astype(F32)
    remote(rgy, rgy, send_c.at[0], recv_g.at[1], y_mate).wait_recv()
    sgx[...] = (near_g + rgy[...].astype(F32)).astype(BF16)
    for o in (1, 3, 2):
        other = lax.rem(x + o, 4)
        send(sgx.at[other], rgx.at[x], send_gx.at[o - 1], recv_gx.at[x], 4 * other + quarter)
    rgx[x] = sgx[x]
    for o in (1, 3, 2):
        other = lax.rem(x + o, 4)
        remote(rgx.at[other], rgx.at[other], send_c.at[0], recv_gx.at[other], y_mate).wait_recv()
    weights = rgx[0].astype(F32)
    for h in range(1, 4):
        weights = weights + rgx[h].astype(F32)
    guk[...] = weights[:, 0:512]
    guv[...] = weights[:, 512:1024]

    for o in range(1, heads):
        source = lax.rem(head + o, heads)
        remote(ag.at[source], ag.at[source], send_c.at[0], recv_a.at[source], y_mate).wait_recv()
    for p in range(heads):
        gl[piece * p : piece * p + piece, :] = ag[p, :, 0:512].astype(F32)
        packed = ag[p, 0:half, 512:640].astype(F32)
        gr[half * p : half * p + half, :] = packed[:, 0:64]
        gr[128 + half * p : 128 + half * p + half, :] = swap_halves(packed)[:, 0:64]
    for copy in started:
        copy.wait_send()


def reduce(heads, dkv, dq, lat, uk, uv):
    vmem = pl.BlockSpec(memory_space=pltpu.VMEM)
    piece = TOKENS // heads
    dma = pltpu.SemaphoreType.DMA
    return pl.pallas_call(
        functools.partial(reduce_kernel, heads),
        name="reduce",
        out_shape=(
            jax.ShapeDtypeStruct((TOKENS, 512), BF16),
            jax.ShapeDtypeStruct((TOKENS, 256), BF16),
            jax.ShapeDtypeStruct((TOKENS, 512), F32),
            jax.ShapeDtypeStruct((TOKENS, 64), F32),
            jax.ShapeDtypeStruct((32, 512), F32),
            jax.ShapeDtypeStruct((32, 512), F32),
        ),
        in_specs=[vmem] * 5,
        out_specs=(vmem,) * 6,
        scratch_shapes=[
            pltpu.VMEM((8, ROWS, 128), BF16),
            pltpu.VMEM((4, ROWS, 128), BF16),
            pltpu.VMEM((4, ROWS, 128), BF16),
            pltpu.VMEM((4, ROWS, 128), BF16),
            pltpu.VMEM((4, ROWS, 128), BF16),
            pltpu.VMEM((4, DQ_ROWS, 128), BF16),
            pltpu.VMEM((heads, piece, 640), BF16),
            pltpu.VMEM((heads, piece, 640), BF16),
            pltpu.VMEM((heads, piece, 640), BF16),
            pltpu.VMEM((2, 2, 4, 32, 1024), BF16),
            pltpu.VMEM((2, 4, 32, 1024), BF16),
            pltpu.VMEM((4, 32, 1024), BF16),
            pltpu.VMEM((4, 32, 1024), BF16),
            pltpu.VMEM((4, 32, 1024), BF16),
            pltpu.VMEM((4, 32, 1024), BF16),
            dma((8,)), dma((8,)),
            dma((3,)), dma((4,)),
            dma((4,)), dma((4,)),
            dma((3,)), dma((4,)),
            dma((heads,)), dma((heads,)),
            dma((heads,)), dma((heads,)),
            dma((2,)), dma((2,)),
            dma((3,)), dma((4,)),
        ],
        compiler_params=pltpu.CompilerParams(
            collective_id=1, has_side_effects=True, vmem_limit_bytes=40 * MIB
        ),
    )(dkv, dq, lat, uk, uv)


def per_device(q_nope, q_rope, latent, rope_keys, out_grad, up_keys, up_values, group_order):
    kv, qd = exchange(q_nope, q_rope, out_grad, latent, rope_keys, up_keys, up_values)
    dkv, dq = attention(group_order, kv, qd)
    return reduce(lax.axis_size("head"), dkv, dq, latent, up_keys, up_values)


def solution(mesh):
    in_specs = (
        P("ctx", "head"),
        P("ctx", "head"),
        P("ctx", None),
        P("ctx", None),
        P("ctx", "head"),
        P(None, "head"),
        P(None, "head"),
        P(),
    )
    out_specs = (
        P("ctx", "head"),
        P("ctx", "head"),
        P("ctx", None),
        P("ctx", None),
        P("ctx", "head"),
        P("ctx", "head"),
    )
    return jax.shard_map(
        per_device, mesh=mesh, in_specs=in_specs, out_specs=out_specs, check_vma=False
    )
```

```python
import functools
import math

import jax
import jax.numpy as jnp
from jax import lax
from jax.experimental import pallas as pl
from jax.experimental.pallas import tpu as pltpu
from jax.sharding import PartitionSpec as P

MESH = pl.DeviceIdType.MESH
F32 = jnp.float32
BF16 = jnp.bfloat16

SCALE = (128 + 64) ** (-0.5)
EXP2_SCALE = SCALE * math.log2(math.e)
NEG_LARGE = -1e30

GROUP = 128
GROUPS = 32
BLOCKS = 16
TOKENS = 256
ROWS = 640
DQ_ROWS = 384
MIB = 1024 * 1024

NT = (((1,), (1,)), ((), ()))
TN = (((0,), (0,)), ((), ()))


def low_lanes(rows):
    return lax.broadcasted_iota(jnp.int32, (rows, 128), 1) < 64


def swap_halves(tile):
    return pltpu.roll(tile, 64, 1)


def place_of(me):
    x = lax.div(me, 4)
    quarter = lax.rem(me, 4)
    core = lax.rem(quarter, 2)
    y = lax.div(quarter, 2)
    y_mate = 4 * x + 2 * (1 - y) + core
    core_mate = 4 * x + 2 * y + (1 - core)
    return x, quarter, y, core, y_mate, core_mate


def remote(src, dst, send_sem, recv_sem, ctx):
    return pltpu.make_async_remote_copy(
        src_ref=src,
        dst_ref=dst,
        send_sem=send_sem,
        recv_sem=recv_sem,
        device_id={"ctx": ctx},
        device_id_type=MESH,
    )


def fused_kernel(
    heads, order, qn_in, qr_in, og_in, lat_in, rope_in, uk_in, uv_in,
    gqn, gqr, gl, gr, guk, guv,
    qn, qr, og, rope, uk, uv, skv, sq, kv, qd, lats,
    rm, kt, qm, qct, doct, s_all, dp_all, tops, stats, dqt,
    dkv, rc, sy, ry, rx, sdq, rdq, wsum, gp, gc, sgy, rgy, sgx, rgx, sl, rl, ag,
    load_sem, s_kvx, s_kvy, s_kvc, r_kv, s_q, r_q, s_lat, r_lat,
    s_c, r_c, s_y, r_y, s_x, r_x, s_dq, r_dq, s_g, r_g, s_gx, r_gx, s_l, r_l, s_a, r_a,
):
    me = lax.axis_index("ctx")
    head = lax.axis_index("head")
    x, quarter, y, core, y_mate, core_mate = place_of(me)
    piece = TOKENS // heads

    def at_x(o):
        return lax.rem(x + o, 4)

    loads = [
        pltpu.make_async_copy(src, dst, load_sem.at[n])
        for n, (src, dst) in enumerate(
            (
                (lat_in, lats.at[x]), (uk_in, uk), (uv_in, uv), (rope_in, rope),
                (qn_in, qn), (qr_in, qr), (og_in, og),
            )
        )
    ]
    for copy in loads:
        copy.start()

    barrier = pltpu.get_barrier_semaphore()
    for o in (1, 2, 3):
        pl.semaphore_signal(
            barrier, inc=1, device_id={"ctx": 4 * at_x(o) + quarter}, device_id_type=MESH
        )
    for mate in (y_mate, core_mate):
        pl.semaphore_signal(barrier, inc=1, device_id={"ctx": mate}, device_id_type=MESH)
    for o in range(1, heads):
        pl.semaphore_signal(
            barrier, inc=1, device_id={"head": lax.rem(head + o, heads)}, device_id_type=MESH
        )

    started = []

    def send(*args):
        copy = remote(*args)
        copy.start()
        started.append(copy)

    def wait_recv(ref, sem):
        remote(ref, ref, s_c.at[0], sem, core_mate).wait_recv()

    for copy in loads[0:4]:
        copy.wait()
    latent = lats[x]
    keys = jnp.dot(latent, uk[...], preferred_element_type=F32).astype(BF16)
    values = jnp.dot(latent, uv[...], preferred_element_type=F32).astype(BF16)
    rope_t = rope[...].astype(F32)
    packed_rope = jnp.concatenate([rope_t[:, 0:128], rope_t[:, 128:256]], axis=0).T.astype(BF16)
    for h in range(4):
        skv[h, 0:256, :] = keys[:, 128 * h : 128 * h + 128]
        skv[h, 256:512, :] = values[:, 128 * h : 128 * h + 128]
        skv[h, 512:640, :] = packed_rope
    pl.semaphore_wait(barrier, 5 + heads - 1)

    def send_kv(o):
        send(skv.at[at_x(o)], kv.at[me], s_kvx.at[o - 1], r_kv.at[me], 4 * at_x(o) + quarter)

    def send_q(o):
        send(sq.at[at_x(o)], qd.at[x], s_q.at[o - 1], r_q.at[x], 4 * at_x(o) + quarter)

    send_kv(1)
    send_kv(3)
    send(skv.at[x], kv.at[me], s_kvy.at[0], r_kv.at[me], y_mate)
    send(skv.at[x], kv.at[me], s_kvc.at[0], r_kv.at[me], core_mate)
    low = low_lanes(128)
    for copy in loads[4:7]:
        copy.wait()
    for h in range(4):
        sq[h, 0:256, :] = qn[:, 128 * h : 128 * h + 128]
        sq[h, 256:512, :] = og[:, 128 * h : 128 * h + 128]
        tile = qr[:, 128 * (h // 2) : 128 * (h // 2) + 128].astype(F32)
        top, bottom = tile[0:128], tile[128:256]
        if h % 2 == 0:
            packed = jnp.where(low, top, swap_halves(bottom))
        else:
            packed = jnp.where(low, swap_halves(top), bottom)
        sq[h, 512:640, :] = packed.astype(BF16)
    send_q(1)
    send_q(3)
    send_kv(2)
    send_q(2)
    kv[me] = skv[x]
    qd[x] = sq[x]

    lane = lax.broadcasted_iota(jnp.int32, (128, 128), 1)

    def prepare_keys(block):
        packed = kv[block, 512:640, :].astype(F32)
        for half in range(2):
            place = order[2 * block + half]
            hidden = jnp.where(lane < 64 + place, NEG_LARGE, 0.0)
            hidden = jnp.where(lane < 96, hidden, 0.0)
            rows = packed if half == 0 else swap_halves(packed)
            rm[block, 128 * half : 128 * half + 128, :] = jnp.where(low, rows, hidden).astype(BF16)
        kt[block, 0:128, :] = kv[block, 0:256, :].T
        kt[block, 128:256, :] = rm[block].T

    def prepare_queries(slot):
        packed = qd[slot, 512:640, :].astype(F32)
        for half in range(2):
            place = order[2 * (4 * slot + quarter) + half]
            chosen = jnp.where(lane == 64 + place, 1.0, 0.0)
            rows = packed if half == 0 else swap_halves(packed)
            qm[slot, 128 * half : 128 * half + 128, :] = jnp.where(low, rows, chosen).astype(BF16)
        qct[slot, 0:128, :] = qd[slot, 0:256, :].T
        qct[slot, 128:256, :] = qm[slot].T
        doct[slot] = qd[slot, 256:512, :].T
        tops[slot] = jnp.full((8, 256), NEG_LARGE, F32)

    def scores(key_x, query_x):
        top = tops[query_x]
        for b in range(4):
            block = 4 * key_x + lax.rem(quarter + b, 4)
            keys_in = jnp.concatenate([kv[block, 0:256, :], rm[block]], axis=1)
            s = jnp.dot(keys_in, qct[query_x], preferred_element_type=F32)
            if b == 0:
                rows = lax.broadcasted_iota(jnp.int32, (256, 256), 0)
                columns = lax.broadcasted_iota(jnp.int32, (256, 256), 1)
                limit = jnp.where(key_x == query_x, 0, 1024)
                same = (rows < 128) == (columns < 128)
                s = jnp.where(same & (rows > columns + limit), NEG_LARGE, s)
            s_all[query_x, block] = s
            top = jnp.maximum(top, jnp.max(s.reshape(32, 8, 256), axis=0))
            dp_all[query_x, block] = jnp.dot(
                kv[block, 256:512, :], doct[query_x], preferred_element_type=F32
            )
        tops[query_x] = top

    def take_x(o, n):
        block = 4 * at_x(o) + quarter
        wait_recv(kv.at[block], r_kv.at[block])
        send(kv.at[block], kv.at[block], s_kvy.at[n], r_kv.at[block], y_mate)
        send(kv.at[block], kv.at[block], s_kvc.at[n], r_kv.at[block], core_mate)

    def take_y(o, n):
        block = 4 * at_x(o) + 2 * (1 - y) + core
        wait_recv(kv.at[block], r_kv.at[block])
        send(kv.at[block], kv.at[block], s_kvc.at[n], r_kv.at[block], core_mate)

    def take_set(o, n):
        take_y(o, n)
        for side in range(2):
            block = 4 * at_x(o) + 2 * side + (1 - core)
            wait_recv(kv.at[block], r_kv.at[block])

        @pl.loop(0, 4)
        def _(b):
            prepare_keys(4 * at_x(o) + b)

    def take_queries(o):
        wait_recv(qd.at[at_x(o)], r_q.at[at_x(o)])
        prepare_queries(at_x(o))

    prepare_queries(x)
    take_x(1, 1)
    take_x(3, 2)
    take_set(0, 4)
    scores(x, x)
    take_set(1, 5)
    scores(at_x(1), x)
    take_queries(1)

    @pl.loop(0, 2)
    def _(n):
        scores(at_x(n), at_x(1))

    take_x(2, 3)
    take_queries(3)

    @pl.loop(0, 2)
    def _(n):
        scores(at_x(n), at_x(3))

    take_set(3, 6)

    @pl.loop(0, 3)
    def _(n):
        scores(at_x(3), at_x(n + lax.div(n, 2)))

    take_queries(2)
    for o in (1, 3, 2):
        send(lats.at[x], lats.at[x], s_lat.at[o - 1], r_lat.at[x], 4 * at_x(o) + quarter)

    @pl.loop(0, 3)
    def _(n):
        scores(at_x(n + lax.div(n, 2)), at_x(2))

    take_set(2, 7)

    @pl.loop(0, 4)
    def _(n):
        scores(at_x(2), at_x(n))

    @pl.loop(0, 4)
    def _(i):
        top = jnp.max(tops[i], axis=0, keepdims=True) * EXP2_SCALE

        @pl.loop(0, 4, init_carry=(jnp.zeros((8, 256), F32), jnp.zeros((8, 256), F32)))
        def sums(n, carry):
            total, weighted = carry
            for b in range(4):
                block = 4 * n + b
                p = jnp.exp2(s_all[i, block] * EXP2_SCALE - top)
                s_all[i, block] = p
                total = total + jnp.sum(p.reshape(32, 8, 256), axis=0)
                weighted = weighted + jnp.sum((p * dp_all[i, block]).reshape(32, 8, 256), axis=0)
            return total, weighted

        inverse = 1.0 / jnp.sum(sums[0], axis=0, keepdims=True)
        stats[0, i] = inverse
        stats[1, i] = jnp.sum(sums[1], axis=0, keepdims=True) * inverse
        dqt[i] = jnp.zeros((256, 256), F32)

    def grads(first, second):
        blocks = (first, second)
        dk = [jnp.zeros((256, 256), F32)] * 2
        dv = [jnp.zeros((256, 128), F32)] * 2
        for i in range(4):
            inverse, delta = stats[0, i], stats[1, i]
            queries = jnp.concatenate([qd[i, 0:256, :], qm[i]], axis=1)
            ds = []
            for n, block in enumerate(blocks):
                attn = s_all[i, block] * inverse
                ds.append((attn * (dp_all[i, block] - delta)).astype(BF16))
                dv[n] = dv[n] + jnp.dot(
                    attn.astype(BF16), qd[i, 256:512, :], preferred_element_type=F32
                )
                dk[n] = dk[n] + jnp.dot(ds[n], queries, preferred_element_type=F32)
            keys_t = jnp.concatenate([kt[first], kt[second]], axis=1)
            dqt[i] += jnp.dot(keys_t, jnp.concatenate(ds, axis=0), preferred_element_type=F32)
        for n, block in enumerate(blocks):
            scaled = dk[n] * SCALE
            dkv[block, 0:256, :] = scaled[:, 0:128].astype(BF16)
            dkv[block, 256:512, :] = dv[n].astype(BF16)
            tail = scaled[:, 128:256]
            dkv[block, 512:640, :] = jnp.where(low, tail[0:128], swap_halves(tail[128:256])).astype(
                BF16
            )

    def to_core(slot, block):
        return remote(dkv.at[block], rc.at[slot], s_c.at[slot], r_c.at[slot], core_mate)

    def to_y(other):
        return remote(sy.at[other], ry.at[other], s_y.at[other], r_y.at[other], y_mate)

    def pass_far(other):
        wait_recv(rc.at[other], r_c.at[other])
        mine = dkv[4 * other + 2 * (1 - y) + core].astype(F32)
        sy[other] = (mine + rc[other].astype(F32)).astype(BF16)
        to_y(other).start()

    @pl.loop(0, 8)
    def _(n):
        near = lax.div(n, 4)
        other = at_x(1 + lax.rem(n, 4))
        side = near * y + (1 - near) * (1 - y)
        out = 4 * other + 2 * side + (1 - core)
        grads(out, 4 * other + 2 * side + core)
        to_core(4 * near + other, out).start()

        @pl.when((n > 0) & (n < 5))
        def _():
            pass_far(at_x(n))

    for i in range(4):
        whole = dqt[i].T * SCALE
        sdq[i, 0:256, :] = whole[:, 0:128].astype(BF16)
        tail = whole[:, 128:256]
        sdq[i, 256:384, :] = jnp.where(low, tail[0:128], swap_halves(tail[128:256])).astype(BF16)
    rdq[x] = sdq[x]

    for o in (1, 2, 3, 0):
        other = at_x(o)
        wait_recv(rc.at[4 + other], r_c.at[4 + other])
        block = 4 * other + 2 * y + core
        near = dkv[block].astype(F32) + rc[4 + other].astype(F32)
        wait_recv(ry.at[other], r_y.at[other])
        full = (near + ry[other].astype(F32)).astype(BF16)
        dkv[block] = full
        if o:
            send(dkv.at[block], rx.at[x], s_x.at[o - 1], r_x.at[x], 4 * other + quarter)
            wait_recv(lats.at[other], r_lat.at[other])
        else:
            rx[x] = full
        pair = jnp.concatenate([full[0:256], full[256:512]], axis=1)
        term = lax.dot_general(lats[other], pair, TN, preferred_element_type=F32)
        if o == 1:
            wsum[...] = term
        elif o:
            wsum[...] += term
        else:
            total = (wsum[...] + term).astype(BF16)
        if o == 3:
            for oo in (1, 3, 2):
                send(
                    sdq.at[at_x(oo)], rdq.at[x], s_dq.at[oo - 1], r_dq.at[x], 4 * at_x(oo) + quarter
                )

    for cc in range(2):
        for yy in range(2):
            for xx in range(4):
                row = 32 * (4 * xx + 2 * yy + cc)
                gp[cc, yy, xx] = total[row : row + 32]
    send(gp.at[1 - core], gc, s_g.at[0], r_g.at[0], core_mate)

    def latent_term(h):
        columns = pl.ds(pl.multiple_of(128 * h, 128), 128)
        term = lax.dot_general(rx[h, 0:256, :], uk[:, columns], NT, preferred_element_type=F32)
        return term + lax.dot_general(
            rx[h, 256:512, :], uv[:, columns], NT, preferred_element_type=F32
        )

    summed = latent_term(x)
    turned = rx[x, 512:640, :].astype(F32)
    for o in (3, 2, 1):
        wait_recv(rx.at[at_x(o)], r_x.at[at_x(o)])
        summed = summed + latent_term(at_x(o))
        turned = turned + rx[at_x(o), 512:640, :].astype(F32)
    half = piece // 2
    for p in range(heads):
        sl[p, :, 0:512] = summed[piece * p : piece * p + piece].astype(BF16)
        sl[p, 0:half, 512:640] = turned[half * p : half * p + half].astype(BF16)
        sl[p, half:piece, 512:640] = jnp.zeros((piece - half, 128), BF16)

    def send_head(src, dst, send_sem, recv_sem, to):
        copy = pltpu.make_async_remote_copy(
            src_ref=src,
            dst_ref=dst,
            send_sem=send_sem,
            recv_sem=recv_sem,
            device_id={"head": to},
            device_id_type=MESH,
        )
        copy.start()
        started.append(copy)

    for o in range(1, heads):
        to = lax.rem(head + o, heads)
        send_head(sl.at[to], rl.at[head], s_l.at[o], r_l.at[head], to)
    rl[head] = sl[head]

    wait_recv(gc, r_g.at[0])
    sgy[...] = (gp[core, 1 - y].astype(F32) + gc[1 - y].astype(F32)).astype(BF16)
    send(sgy, rgy, s_g.at[1], r_g.at[1], y_mate)
    near_g = gp[core, y].astype(F32) + gc[y].astype(F32)

    for o in (1, 2, 3):
        wait_recv(rdq.at[at_x(o)], r_dq.at[at_x(o)])
    for h in range(4):
        gqn[:, 128 * h : 128 * h + 128] = rdq[h, 0:256, :]
    for two in range(2):
        a = rdq[2 * two, 256:384, :].astype(F32)
        b = rdq[2 * two + 1, 256:384, :].astype(F32)
        cols = slice(128 * two, 128 * two + 128)
        gqr[0:128, cols] = jnp.where(low, a, swap_halves(b)).astype(BF16)
        gqr[128:256, cols] = jnp.where(low, swap_halves(a), b).astype(BF16)

    wait_recv(rgy, r_g.at[1])
    sgx[...] = (near_g + rgy[...].astype(F32)).astype(BF16)
    for o in (1, 3, 2):
        send(sgx.at[at_x(o)], rgx.at[x], s_gx.at[o - 1], r_gx.at[x], 4 * at_x(o) + quarter)
    rgx[x] = sgx[x]

    for o in range(1, heads):
        source = lax.rem(head + o, heads)
        wait_recv(rl.at[source], r_l.at[source])
    over_heads = rl[0].astype(F32)
    for p in range(1, heads):
        over_heads = over_heads + rl[p].astype(F32)
    ag[head] = over_heads.astype(BF16)
    for o in range(1, heads):
        to = lax.rem(head + o, heads)
        send_head(ag.at[head], ag.at[head], s_a.at[o], r_a.at[head], to)

    for o in (1, 2, 3):
        wait_recv(rgx.at[at_x(o)], r_gx.at[at_x(o)])
    for h in range(4):
        guk[:, 128 * h : 128 * h + 128] = rgx[h, :, 0:128].astype(F32)
        guv[:, 128 * h : 128 * h + 128] = rgx[h, :, 128:256].astype(F32)

    for o in range(1, heads):
        source = lax.rem(head + o, heads)
        wait_recv(ag.at[source], r_a.at[source])
    packed = []
    for p in range(heads):
        gl[piece * p : piece * p + piece, :] = ag[p, :, 0:512].astype(F32)
        packed.append(ag[p, 0:half, 512:640].astype(F32))
    turned_t = jnp.concatenate(packed, axis=0).T
    gr[:, 0:128] = turned_t[0:64]
    gr[:, 128:256] = turned_t[64:128]

    for copy in started:
        copy.wait_send()
    for other in range(4):
        to_y(other).wait_send()
        to_core(other, other).wait_send()
        to_core(4 + other, other).wait_send()


def fused(heads, order, qn, qr, og, lat, rope_t, uk, uv):
    hbm = pl.BlockSpec(memory_space=pltpu.HBM)
    vmem = pl.BlockSpec(memory_space=pltpu.VMEM)
    piece = TOKENS // heads
    dma = pltpu.SemaphoreType.DMA
    bf = lambda *shape: pltpu.VMEM(shape, BF16)
    f32 = lambda *shape: pltpu.VMEM(shape, F32)
    return pl.pallas_call(
        functools.partial(fused_kernel, heads),
        name="fused",
        out_shape=(
            jax.ShapeDtypeStruct((TOKENS, 512), BF16),
            jax.ShapeDtypeStruct((TOKENS, 256), BF16),
            jax.ShapeDtypeStruct((TOKENS, 512), F32),
            jax.ShapeDtypeStruct((64, TOKENS), F32),
            jax.ShapeDtypeStruct((32, 512), F32),
            jax.ShapeDtypeStruct((32, 512), F32),
        ),
        in_specs=[pl.BlockSpec(memory_space=pltpu.SMEM)] + [hbm] * 7,
        out_specs=(vmem,) * 6,
        scratch_shapes=[
            bf(256, 512), bf(256, 256), bf(256, 512), bf(64, 256), bf(512, 512), bf(512, 512),
            bf(4, ROWS, 128), bf(4, ROWS, 128), bf(BLOCKS, ROWS, 128), bf(4, ROWS, 128),
            bf(4, 256, 512),
            bf(BLOCKS, 256, 128), bf(BLOCKS, 256, 256), bf(4, 256, 128), bf(4, 256, 256),
            bf(4, 128, 256),
            f32(4, BLOCKS, 256, 256), f32(4, BLOCKS, 256, 256), f32(4, 8, 256), f32(2, 4, 1, 256),
            f32(4, 256, 256),
            bf(BLOCKS, ROWS, 128), bf(8, ROWS, 128), bf(4, ROWS, 128), bf(4, ROWS, 128),
            bf(4, ROWS, 128), bf(4, DQ_ROWS, 128), bf(4, DQ_ROWS, 128),
            f32(512, 256),
            bf(2, 2, 4, 32, 256), bf(2, 4, 32, 256), bf(4, 32, 256), bf(4, 32, 256),
            bf(4, 32, 256), bf(4, 32, 256),
            bf(heads, piece, 640), bf(heads, piece, 640), bf(heads, piece, 640),
            dma((7,)), dma((3,)), dma((4,)), dma((8,)), dma((BLOCKS,)), dma((3,)), dma((4,)),
            dma((3,)), dma((4,)),
            dma((8,)), dma((8,)), dma((4,)), dma((4,)), dma((3,)), dma((4,)), dma((3,)), dma((4,)),
            dma((2,)), dma((2,)), dma((3,)), dma((4,)),
            dma((heads,)), dma((heads,)), dma((heads,)), dma((heads,)),
        ],
        compiler_params=pltpu.CompilerParams(
            collective_id=0, has_side_effects=True, vmem_limit_bytes=60 * MIB
        ),
    )(order, qn, qr, og, lat, rope_t, uk, uv)


def finish_kernel(*refs):
    sources, results, sems = refs[0:6], refs[6:12], refs[12]
    copies = [
        pltpu.make_async_copy(src, dst, sems.at[n]) for n, (src, dst) in enumerate(zip(sources, results))
    ]
    for copy in copies:
        copy.start()
    for copy in copies:
        copy.wait()


def finish(*arrays):
    vmem = pl.BlockSpec(memory_space=pltpu.VMEM)
    hbm = pl.BlockSpec(memory_space=pltpu.HBM)
    return pl.pallas_call(
        finish_kernel,
        name="finish",
        out_shape=tuple(jax.ShapeDtypeStruct(a.shape, a.dtype) for a in arrays),
        in_specs=[vmem] * 6,
        out_specs=(hbm,) * 6,
        scratch_shapes=[pltpu.SemaphoreType.DMA((6,))],
    )(*arrays)


def per_device(q_nope, q_rope, latent, rope_keys, out_grad, up_keys, up_values, group_order):
    outs = fused(
        lax.axis_size("head"), group_order, q_nope, q_rope, out_grad, latent, rope_keys.T,
        up_keys, up_values,
    )
    outs = finish(*outs)
    return (outs[0], outs[1], outs[2], outs[3].T, outs[4], outs[5])


def solution(mesh):
    in_specs = (
        P("ctx", "head"),
        P("ctx", "head"),
        P("ctx", None),
        P("ctx", None),
        P("ctx", "head"),
        P(None, "head"),
        P(None, "head"),
        P(),
    )
    out_specs = (
        P("ctx", "head"),
        P("ctx", "head"),
        P("ctx", None),
        P("ctx", None),
        P("ctx", "head"),
        P("ctx", "head"),
    )
    return jax.shard_map(
        per_device, mesh=mesh, in_specs=in_specs, out_specs=out_specs, check_vma=False
    )
```

```python
import functools
import math

import jax
import jax.numpy as jnp
from jax import lax
from jax.experimental import pallas as pl
from jax.experimental.pallas import tpu as pltpu
from jax.sharding import PartitionSpec as P

MESH = pl.DeviceIdType.MESH
F32 = jnp.float32
BF16 = jnp.bfloat16

SCALE = (128 + 64) ** (-0.5)
EXP2_SCALE = SCALE * math.log2(math.e)
NEG_LARGE = -1e30

GROUP = 128
GROUPS = 32
BLOCKS = 16
TOKENS = 256
ROWS = 640
DQ_ROWS = 384
MIB = 1024 * 1024

NT = (((1,), (1,)), ((), ()))
TN = (((0,), (0,)), ((), ()))


def low_lanes(rows):
    return lax.broadcasted_iota(jnp.int32, (rows, 128), 1) < 64


def swap_halves(tile):
    return pltpu.roll(tile, 64, 1)


def place_of(me):
    x = lax.div(me, 4)
    quarter = lax.rem(me, 4)
    core = lax.rem(quarter, 2)
    y = lax.div(quarter, 2)
    y_mate = 4 * x + 2 * (1 - y) + core
    core_mate = 4 * x + 2 * y + (1 - core)
    return x, quarter, y, core, y_mate, core_mate


def remote(src, dst, send_sem, recv_sem, ctx):
    return pltpu.make_async_remote_copy(
        src_ref=src,
        dst_ref=dst,
        send_sem=send_sem,
        recv_sem=recv_sem,
        device_id={"ctx": ctx},
        device_id_type=MESH,
    )


def fused_kernel(
    heads, order, qn_in, qr_in, og_in, lat_in, rope_in, uk_in, uv_in,
    gqn, gqr, gl, gr, guk, guv,
    qn, qr, og, rope, uk, uv, skv, sq, kv, qd, lats,
    rm, kt, qm, qct, doct, s_all, dp_all, stats, dqt,
    dkv, rc, sy, ry, rx, sdq, rdq, wsum, gp, gc, sgy, rgy, sgx, rgx, sl, rl, ag,
    load_sem, s_kvx, s_kvy, s_kvc, r_kv, s_q, r_q, s_lat, r_lat,
    s_c, r_c, s_y, r_y, s_x, r_x, s_dq, r_dq, s_g, r_g, s_gx, r_gx, s_l, r_l, s_a, r_a,
):
    me = lax.axis_index("ctx")
    head = lax.axis_index("head")
    x, quarter, y, core, y_mate, core_mate = place_of(me)
    z = lax.rem(head, 4)
    piece = TOKENS // heads

    def at_x(o):
        return lax.rem(x + o, 4)

    loads = [
        pltpu.make_async_copy(src, dst, load_sem.at[n])
        for n, (src, dst) in enumerate(
            (
                *((lat_in.at[:, pl.ds(128 * k, 128)], lats.at[k, x]) for k in range(4)),
                (uk_in, uk), (uv_in, uv), (rope_in, rope), (qn_in, qn), (qr_in, qr), (og_in, og),
            )
        )
    ]
    for copy in loads:
        copy.start()

    barrier = pltpu.get_barrier_semaphore()
    for o in (1, 2, 3):
        pl.semaphore_signal(
            barrier, inc=1, device_id={"ctx": 4 * at_x(o) + quarter}, device_id_type=MESH
        )
    for mate in (y_mate, core_mate):
        pl.semaphore_signal(barrier, inc=1, device_id={"ctx": mate}, device_id_type=MESH)
    for o in range(1, heads):
        pl.semaphore_signal(
            barrier, inc=1, device_id={"head": lax.rem(head + o, heads)}, device_id_type=MESH
        )

    started = []

    def send(*args):
        copy = remote(*args)
        copy.start()
        started.append(copy)

    def send_head(src, dst, send_sem, recv_sem, to):
        copy = pltpu.make_async_remote_copy(
            src_ref=src,
            dst_ref=dst,
            send_sem=send_sem,
            recv_sem=recv_sem,
            device_id={"head": to},
            device_id_type=MESH,
        )
        copy.start()
        started.append(copy)

    def wait_recv(ref, sem):
        remote(ref, ref, s_c.at[0], sem, core_mate).wait_recv()

    for copy in loads[0:7]:
        copy.wait()

    def latent_rows(block_x):
        return jnp.concatenate([lats[k, block_x] for k in range(4)], axis=1)

    latent = latent_rows(x)
    keys = jnp.dot(latent, uk[...], preferred_element_type=F32).astype(BF16)
    values = jnp.dot(latent, uv[...], preferred_element_type=F32).astype(BF16)
    rope_t = rope[...].astype(F32)
    packed_rope = jnp.concatenate([rope_t[:, 0:128], rope_t[:, 128:256]], axis=0).T.astype(BF16)
    for h in range(4):
        skv[h, 0:256, :] = keys[:, 128 * h : 128 * h + 128]
        skv[h, 256:384, :] = packed_rope
        skv[h, 384:640, :] = values[:, 128 * h : 128 * h + 128]
    pl.semaphore_wait(barrier, 5 + heads - 1)

    parts = (pl.ds(0, 384), pl.ds(384, 256))

    def send_block(ref, block, sem, n, ctx):
        for m, rows in enumerate(parts):
            send(
                ref.at[rows], kv.at[block, rows], sem.at[2 * n + m], r_kv.at[2 * block + m], ctx
            )

    def wait_block(block):
        for m, rows in enumerate(parts):
            wait_recv(kv.at[block, rows], r_kv.at[2 * block + m])

    def send_kv(o):
        send_block(skv.at[at_x(o)], me, s_kvx, o - 1, 4 * at_x(o) + quarter)

    def send_q(o):
        send(sq.at[at_x(o)], qd.at[x], s_q.at[o - 1], r_q.at[x], 4 * at_x(o) + quarter)

    send_kv(1)
    send_kv(3)
    send_block(skv.at[x], me, s_kvy, 0, y_mate)
    send_block(skv.at[x], me, s_kvc, 0, core_mate)
    low = low_lanes(128)
    for copy in loads[7:10]:
        copy.wait()
    for h in range(4):
        sq[h, 0:256, :] = qn[:, 128 * h : 128 * h + 128]
        sq[h, 256:512, :] = og[:, 128 * h : 128 * h + 128]
        tile = qr[:, 128 * (h // 2) : 128 * (h // 2) + 128].astype(F32)
        top, bottom = tile[0:128], tile[128:256]
        if h % 2 == 0:
            packed = jnp.where(low, top, swap_halves(bottom))
        else:
            packed = jnp.where(low, swap_halves(top), bottom)
        sq[h, 512:640, :] = packed.astype(BF16)
    send_q(1)
    send_q(3)
    send_kv(2)
    send_q(2)
    kv[me] = skv[x]
    qd[x] = sq[x]

    lane = lax.broadcasted_iota(jnp.int32, (128, 128), 1)

    def prepare_keys(block):
        packed = kv[block, 256:384, :].astype(F32)
        for half in range(2):
            place = order[2 * block + half]
            hidden = jnp.where(lane < 64 + place, NEG_LARGE, 0.0)
            hidden = jnp.where(lane < 96, hidden, 0.0)
            rows = packed if half == 0 else swap_halves(packed)
            rm[block, 128 * half : 128 * half + 128, :] = jnp.where(low, rows, hidden).astype(BF16)
        kt[block, 0:128, :] = kv[block, 0:256, :].T
        kt[block, 128:256, :] = rm[block].T

    def prepare_queries(slot):
        packed = qd[slot, 512:640, :].astype(F32)
        for half in range(2):
            place = order[2 * (4 * slot + quarter) + half]
            chosen = jnp.where(lane == 64 + place, 1.0, 0.0)
            rows = packed if half == 0 else swap_halves(packed)
            qm[slot, 128 * half : 128 * half + 128, :] = jnp.where(low, rows, chosen).astype(BF16)
        qct[slot, 0:128, :] = qd[slot, 0:256, :].T
        qct[slot, 128:256, :] = qm[slot].T
        doct[slot] = qd[slot, 256:512, :].T

    def scores(key_x, side, query_x, diagonal=False):
        slot = 2 * key_x + side
        pair = [4 * key_x + 2 * side + core, 4 * key_x + 2 * side + (1 - core)]
        raw, grown = [], []
        for n, block in enumerate(pair):
            keys_in = jnp.concatenate([kv[block, 0:256, :], rm[block]], axis=1)
            score = jnp.dot(keys_in, qct[query_x], preferred_element_type=F32)
            if n == 0 and diagonal:
                rows = lax.broadcasted_iota(jnp.int32, (256, 256), 0)
                columns = lax.broadcasted_iota(jnp.int32, (256, 256), 1)
                limit = jnp.where(key_x == query_x, 0, 1024)
                same = (rows < 128) == (columns < 128)
                score = jnp.where(same & (rows > columns + limit), NEG_LARGE, score)
            raw.append(score)
            dp = jnp.dot(kv[block, 384:640, :], doct[query_x], preferred_element_type=F32)
            dp_all[query_x, block] = dp
            grown.append(dp)
        tops = [jnp.max(score.reshape(32, 8, 256), axis=0) for score in raw]
        top = jnp.max(jnp.maximum(tops[0], tops[1]), axis=0, keepdims=True) * EXP2_SCALE
        total = jnp.zeros((8, 256), F32)
        weighted = jnp.zeros((8, 256), F32)
        for block, score, dp in zip(pair, raw, grown):
            p = jnp.exp2(score * EXP2_SCALE - top)
            s_all[query_x, block] = p
            total = total + jnp.sum(p.reshape(32, 8, 256), axis=0)
            weighted = weighted + jnp.sum((p * dp).reshape(32, 8, 256), axis=0)
        stats[0, query_x, slot] = top
        stats[1, query_x, slot] = jnp.sum(total, axis=0, keepdims=True)
        stats[2, query_x, slot] = jnp.sum(weighted, axis=0, keepdims=True)

    def take_x(o, n):
        block = 4 * at_x(o) + quarter
        for m, rows in enumerate(parts):
            wait_recv(kv.at[block, rows], r_kv.at[2 * block + m])
            for sem, mate in ((s_kvy, y_mate), (s_kvc, core_mate)):
                send(
                    kv.at[block, rows], kv.at[block, rows], sem.at[2 * n + m],
                    r_kv.at[2 * block + m], mate,
                )

    def take_y(o, n):
        block = 4 * at_x(o) + 2 * (1 - y) + core
        wait_block(block)
        send_block(kv.at[block], block, s_kvc, n, core_mate)

    def take_core(o, side):
        block = 4 * at_x(o) + 2 * side + (1 - core)
        wait_block(block)
        prepare_keys(4 * at_x(o) + 2 * side + core)
        prepare_keys(block)

    def take_queries(o):
        wait_recv(qd.at[at_x(o)], r_q.at[at_x(o)])
        prepare_queries(at_x(o))

    far = 1 - y
    prepare_queries(x)
    take_core(0, y)
    scores(x, y, x, True)
    take_x(1, 1)
    take_x(3, 2)
    take_y(0, 4)
    take_core(1, y)
    scores(at_x(1), y, x)
    take_core(3, y)
    scores(at_x(3), y, x)
    take_core(0, far)
    scores(x, far, x)
    take_queries(1)
    take_queries(3)

    for n in range(2):
        for o in (0, 1, 3):
            scores(at_x(o), y, at_x(1 + 2 * n), True)

    take_y(1, 5)
    take_x(2, 3)

    for n in range(2):
        scores(x, far, at_x(1 + 2 * n))

    take_core(1, far)

    for n in range(3):
        scores(at_x(1), far, at_x(n + n // 2))

    take_core(2, y)

    for n in range(3):
        scores(at_x(2), y, at_x(n + n // 2))

    take_y(3, 6)
    take_queries(2)
    for o in (1, 3, 2):
        send(lats.at[z, x], lats.at[z, x], s_lat.at[o - 1], r_lat.at[4 * z + x], 4 * at_x(o) + quarter)
    for o in range(4):
        scores(at_x(o), y, at_x(2), o == 2)
    take_core(3, far)

    for n in range(2):
        scores(at_x(3), far, at_x(2 * n))
        scores(at_x(3), far, at_x(2 * n + 1))

    take_y(2, 7)
    scores(x, far, at_x(2))
    scores(at_x(1), far, at_x(2))
    take_core(2, far)

    for n in range(2):
        scores(at_x(2), far, at_x(2 * n))
        scores(at_x(2), far, at_x(2 * n + 1))

    for n, o in enumerate((1, 3, 2)):
        other = at_x(o)
        wait_recv(lats.at[z, other], r_lat.at[4 * z + other])
        for m, oz in enumerate((1, 3, 2)):
            to = 4 * lax.div(head, 4) + lax.rem(z + oz, 4)
            send_head(
                lats.at[z, other], lats.at[z, other], s_lat.at[3 + 3 * n + m],
                r_lat.at[4 * z + other], to,
            )

    for i in range(4):
        top = stats[0, i, 0]
        for slot in range(1, 8):
            top = jnp.maximum(top, stats[0, i, slot])
        total = jnp.zeros((1, 256), F32)
        weighted = jnp.zeros((1, 256), F32)
        for slot in range(8):
            factor = jnp.exp2(stats[0, i, slot] - top)
            stats[0, i, slot] = factor
            total = total + stats[1, i, slot] * factor
            weighted = weighted + stats[2, i, slot] * factor
        inverse = 1.0 / total
        for slot in range(8):
            stats[0, i, slot] = stats[0, i, slot] * inverse
        stats[1, i, 0] = weighted * inverse
        dqt[i] = jnp.zeros((256, 256), F32)
    wsum[...] = jnp.zeros((512, 256), F32)

    def grads(slot, first, second):
        blocks = (first, second)
        dk = [jnp.zeros((256, 256), F32)] * 2
        dv = [jnp.zeros((256, 128), F32)] * 2
        for i in range(4):
            inverse, delta = stats[0, i, slot], stats[1, i, 0]
            queries = jnp.concatenate([qd[i, 0:256, :], qm[i]], axis=1)
            ds = []
            for n, block in enumerate(blocks):
                attn = s_all[i, block] * inverse
                ds.append((attn * (dp_all[i, block] - delta)).astype(BF16))
                dv[n] = dv[n] + jnp.dot(
                    attn.astype(BF16), qd[i, 256:512, :], preferred_element_type=F32
                )
                dk[n] = dk[n] + jnp.dot(ds[n], queries, preferred_element_type=F32)
            keys_t = jnp.concatenate([kt[first], kt[second]], axis=1)
            dqt[i] += jnp.dot(keys_t, jnp.concatenate(ds, axis=0), preferred_element_type=F32)
        for n, block in enumerate(blocks):
            scaled = dk[n] * SCALE
            dkv[block, 0:256, :] = scaled[:, 0:128].astype(BF16)
            dkv[block, 256:512, :] = dv[n].astype(BF16)
            tail = scaled[:, 128:256]
            dkv[block, 512:640, :] = jnp.where(low, tail[0:128], swap_halves(tail[128:256])).astype(
                BF16
            )

    def to_core(slot, block):
        return remote(dkv.at[block], rc.at[slot], s_c.at[slot], r_c.at[slot], core_mate)

    def to_y(other):
        return remote(sy.at[other], ry.at[other], s_y.at[other], r_y.at[other], y_mate)

    def pass_far(other):
        wait_recv(rc.at[other], r_c.at[other])
        mine = dkv[4 * other + 2 * far + core].astype(F32)
        sy[other] = (mine + rc[other].astype(F32)).astype(BF16)
        to_y(other).start()

    def whole_block(other):
        wait_recv(rc.at[4 + other], r_c.at[4 + other])
        block = 4 * other + 2 * y + core
        near = dkv[block].astype(F32) + rc[4 + other].astype(F32)
        wait_recv(ry.at[other], r_y.at[other])
        full = (near + ry[other].astype(F32)).astype(BF16)
        dkv[block] = full
        return block, full

    def weight_term(other):
        block = 4 * other + 2 * y + core
        pair = jnp.concatenate([dkv[block, 0:256, :], dkv[block, 256:512, :]], axis=1)
        wsum[...] += lax.dot_general(latent_rows(other), pair, TN, preferred_element_type=F32)

    def to_x(n, other, block):
        return remote(dkv.at[block], rx.at[x], s_x.at[n], r_x.at[x], 4 * other + quarter)

    def give_block(n):
        other = at_x(n + 1)
        block, _ = whole_block(other)
        to_x(n, other, block).start()

    @pl.loop(0, 4)
    def _(n):
        other = at_x(1 + n)
        grads(2 * other + far, 4 * other + 2 * far + (1 - core), 4 * other + 2 * far + core)
        to_core(other, 4 * other + 2 * far + (1 - core)).start()
        grads(2 * other + y, 4 * other + 2 * y + (1 - core), 4 * other + 2 * y + core)
        to_core(4 + other, 4 * other + 2 * y + (1 - core)).start()
        pass_far(other)

        @pl.when(n > 0)
        def _():
            give_block(n - 1)

    for i in range(4):
        whole = dqt[i].T * SCALE
        sdq[i, 0:256, :] = whole[:, 0:128].astype(BF16)
        tail = whole[:, 128:256]
        sdq[i, 256:384, :] = jnp.where(low, tail[0:128], swap_halves(tail[128:256])).astype(BF16)
    rdq[x] = sdq[x]
    for o in (1, 3, 2):
        send(sdq.at[at_x(o)], rdq.at[x], s_dq.at[o - 1], r_dq.at[x], 4 * at_x(o) + quarter)

    def latent_term(h):
        columns = pl.ds(pl.multiple_of(128 * h, 128), 128)
        term = lax.dot_general(rx[h, 0:256, :], uk[:, columns], NT, preferred_element_type=F32)
        return term + lax.dot_general(
            rx[h, 256:512, :], uv[:, columns], NT, preferred_element_type=F32
        )

    summed = jnp.zeros((256, 512), F32)
    turned = jnp.zeros((128, 128), F32)
    for o in (3, 2, 0, 1):
        if o:
            wait_recv(rx.at[at_x(o)], r_x.at[at_x(o)])
        else:
            _, full = whole_block(x)
            rx[x] = full
        summed = summed + latent_term(at_x(o))
        turned = turned + rx[at_x(o), 512:640, :].astype(F32)
    half = piece // 2
    for p in range(heads):
        sl[p, :, 0:512] = summed[piece * p : piece * p + piece].astype(BF16)
        sl[p, 0:half, 512:640] = turned[half * p : half * p + half].astype(BF16)
        sl[p, half:piece, 512:640] = jnp.zeros((piece - half, 128), BF16)

    for o in range(1, heads):
        to = lax.rem(head + o, heads)
        send_head(sl.at[to], rl.at[head], s_l.at[o], r_l.at[head], to)
    rl[head] = sl[head]

    for o in (1, 2, 3, 0):
        if o:
            for oz in (1, 2, 3):
                part = lax.rem(z + oz, 4)
                wait_recv(lats.at[part, at_x(o)], r_lat.at[4 * part + at_x(o)])
        weight_term(at_x(o))
    total = wsum[...].astype(BF16)
    for cc in range(2):
        for yy in range(2):
            for xx in range(4):
                row = 32 * (4 * xx + 2 * yy + cc)
                gp[cc, yy, xx] = total[row : row + 32]
    send(gp.at[1 - core], gc, s_g.at[0], r_g.at[0], core_mate)

    wait_recv(gc, r_g.at[0])
    sgy[...] = (gp[core, 1 - y].astype(F32) + gc[1 - y].astype(F32)).astype(BF16)
    send(sgy, rgy, s_g.at[1], r_g.at[1], y_mate)
    near_g = gp[core, y].astype(F32) + gc[y].astype(F32)

    for o in (1, 2, 3):
        wait_recv(rdq.at[at_x(o)], r_dq.at[at_x(o)])
    for h in range(4):
        gqn[:, 128 * h : 128 * h + 128] = rdq[h, 0:256, :]
    for two in range(2):
        a = rdq[2 * two, 256:384, :].astype(F32)
        b = rdq[2 * two + 1, 256:384, :].astype(F32)
        cols = slice(128 * two, 128 * two + 128)
        gqr[0:128, cols] = jnp.where(low, a, swap_halves(b)).astype(BF16)
        gqr[128:256, cols] = jnp.where(low, swap_halves(a), b).astype(BF16)

    wait_recv(rgy, r_g.at[1])
    sgx[...] = (near_g + rgy[...].astype(F32)).astype(BF16)
    for o in (1, 3, 2):
        send(sgx.at[at_x(o)], rgx.at[x], s_gx.at[o - 1], r_gx.at[x], 4 * at_x(o) + quarter)
    rgx[x] = sgx[x]

    for o in range(1, heads):
        source = lax.rem(head + o, heads)
        wait_recv(rl.at[source], r_l.at[source])
    over_heads = rl[0].astype(F32)
    for p in range(1, heads):
        over_heads = over_heads + rl[p].astype(F32)
    ag[head] = over_heads.astype(BF16)
    for o in range(1, heads):
        to = lax.rem(head + o, heads)
        send_head(ag.at[head], ag.at[head], s_a.at[o], r_a.at[head], to)

    for o in (1, 2, 3):
        wait_recv(rgx.at[at_x(o)], r_gx.at[at_x(o)])
    for h in range(4):
        guk[:, 128 * h : 128 * h + 128] = rgx[h, :, 0:128].astype(F32)
        guv[:, 128 * h : 128 * h + 128] = rgx[h, :, 128:256].astype(F32)

    for o in range(1, heads):
        source = lax.rem(head + o, heads)
        wait_recv(ag.at[source], r_a.at[source])
    packed = []
    for p in range(heads):
        gl[piece * p : piece * p + piece, :] = ag[p, :, 0:512].astype(F32)
        packed.append(ag[p, 0:half, 512:640].astype(F32))
    turned_t = jnp.concatenate(packed, axis=0).T
    gr[:, 0:128] = turned_t[0:64]
    gr[:, 128:256] = turned_t[64:128]

    for copy in started:
        copy.wait_send()
    for other in range(4):
        to_core(other, other).wait_send()
        to_core(4 + other, other).wait_send()
    for n in range(4):
        to_y(n).wait_send()
    for n in range(3):
        to_x(n, at_x(n + 1), 0).wait_send()


def fused(heads, order, qn, qr, og, lat, rope_t, uk, uv):
    hbm = pl.BlockSpec(memory_space=pltpu.HBM)
    vmem = pl.BlockSpec(memory_space=pltpu.VMEM)
    piece = TOKENS // heads
    dma = pltpu.SemaphoreType.DMA
    bf = lambda *shape: pltpu.VMEM(shape, BF16)
    f32 = lambda *shape: pltpu.VMEM(shape, F32)
    return pl.pallas_call(
        functools.partial(fused_kernel, heads),
        name="fused",
        out_shape=(
            jax.ShapeDtypeStruct((TOKENS, 512), BF16),
            jax.ShapeDtypeStruct((TOKENS, 256), BF16),
            jax.ShapeDtypeStruct((TOKENS, 512), F32),
            jax.ShapeDtypeStruct((64, TOKENS), F32),
            jax.ShapeDtypeStruct((32, 512), F32),
            jax.ShapeDtypeStruct((32, 512), F32),
        ),
        in_specs=[pl.BlockSpec(memory_space=pltpu.SMEM)] + [hbm] * 7,
        out_specs=(vmem,) * 6,
        scratch_shapes=[
            bf(256, 512), bf(256, 256), bf(256, 512), bf(64, 256), bf(512, 512), bf(512, 512),
            bf(4, ROWS, 128), bf(4, ROWS, 128), bf(BLOCKS, ROWS, 128), bf(4, ROWS, 128),
            bf(4, 4, 256, 128),
            bf(BLOCKS, 256, 128), bf(BLOCKS, 256, 256), bf(4, 256, 128), bf(4, 256, 256),
            bf(4, 128, 256),
            f32(4, BLOCKS, 256, 256), f32(4, BLOCKS, 256, 256), f32(3, 4, 8, 1, 256),
            f32(4, 256, 256),
            bf(BLOCKS, ROWS, 128), bf(8, ROWS, 128), bf(4, ROWS, 128), bf(4, ROWS, 128),
            bf(4, ROWS, 128), bf(4, DQ_ROWS, 128), bf(4, DQ_ROWS, 128),
            f32(512, 256),
            bf(2, 2, 4, 32, 256), bf(2, 4, 32, 256), bf(4, 32, 256), bf(4, 32, 256),
            bf(4, 32, 256), bf(4, 32, 256),
            bf(heads, piece, 640), bf(heads, piece, 640), bf(heads, piece, 640),
            dma((10,)), dma((6,)), dma((8,)), dma((16,)), dma((2 * BLOCKS,)), dma((3,)), dma((4,)),
            dma((12,)), dma((16,)),
            dma((8,)), dma((8,)), dma((4,)), dma((4,)), dma((3,)), dma((4,)), dma((3,)), dma((4,)),
            dma((2,)), dma((2,)), dma((3,)), dma((4,)),
            dma((heads,)), dma((heads,)), dma((heads,)), dma((heads,)),
        ],
        compiler_params=pltpu.CompilerParams(
            collective_id=0, has_side_effects=True, vmem_limit_bytes=60 * MIB
        ),
    )(order, qn, qr, og, lat, rope_t, uk, uv)


def finish_kernel(*refs):
    sources, results, sems = refs[0:6], refs[6:12], refs[12]
    copies = [
        pltpu.make_async_copy(src, dst, sems.at[n]) for n, (src, dst) in enumerate(zip(sources, results))
    ]
    for copy in copies:
        copy.start()
    for copy in copies:
        copy.wait()


def finish(*arrays):
    vmem = pl.BlockSpec(memory_space=pltpu.VMEM)
    hbm = pl.BlockSpec(memory_space=pltpu.HBM)
    return pl.pallas_call(
        finish_kernel,
        name="finish",
        out_shape=tuple(jax.ShapeDtypeStruct(a.shape, a.dtype) for a in arrays),
        in_specs=[vmem] * 6,
        out_specs=(hbm,) * 6,
        scratch_shapes=[pltpu.SemaphoreType.DMA((6,))],
    )(*arrays)


def per_device(q_nope, q_rope, latent, rope_keys, out_grad, up_keys, up_values, group_order):
    outs = fused(
        lax.axis_size("head"), group_order, q_nope, q_rope, out_grad, latent, rope_keys.T,
        up_keys, up_values,
    )
    outs = finish(*outs)
    return (outs[0], outs[1], outs[2], outs[3].T, outs[4], outs[5])


def solution(mesh):
    in_specs = (
        P("ctx", "head"),
        P("ctx", "head"),
        P("ctx", None),
        P("ctx", None),
        P("ctx", "head"),
        P(None, "head"),
        P(None, "head"),
        P(),
    )
    out_specs = (
        P("ctx", "head"),
        P("ctx", "head"),
        P("ctx", None),
        P("ctx", None),
        P("ctx", "head"),
        P("ctx", "head"),
    )
    return jax.shard_map(
        per_device, mesh=mesh, in_specs=in_specs, out_specs=out_specs, check_vma=False
    )
```

```python
import functools
import math

import jax
import jax.numpy as jnp
from jax import lax
from jax.experimental import pallas as pl
from jax.experimental.pallas import tpu as pltpu
from jax.sharding import PartitionSpec as P

MESH = pl.DeviceIdType.MESH
F32 = jnp.float32
BF16 = jnp.bfloat16

SCALE = (128 + 64) ** (-0.5)
EXP2_SCALE = SCALE * math.log2(math.e)
NEG_LARGE = -1e30

GROUP = 128
GROUPS = 32
BLOCKS = 16
TOKENS = 256
ROWS = 640
DQ_ROWS = 384
MIB = 1024 * 1024

NT = (((1,), (1,)), ((), ()))
TN = (((0,), (0,)), ((), ()))


def low_lanes(rows):
    return lax.broadcasted_iota(jnp.int32, (rows, 128), 1) < 64


def swap_halves(tile):
    return pltpu.roll(tile, 64, 1)


def place_of(me):
    x = lax.div(me, 4)
    quarter = lax.rem(me, 4)
    core = lax.rem(quarter, 2)
    y = lax.div(quarter, 2)
    y_mate = 4 * x + 2 * (1 - y) + core
    core_mate = 4 * x + 2 * y + (1 - core)
    return x, quarter, y, core, y_mate, core_mate


def remote(src, dst, send_sem, recv_sem, ctx):
    return pltpu.make_async_remote_copy(
        src_ref=src,
        dst_ref=dst,
        send_sem=send_sem,
        recv_sem=recv_sem,
        device_id={"ctx": ctx},
        device_id_type=MESH,
    )


def fused_kernel(
    heads, order, qn_in, qr_in, og_in, lat_in, rope_in, uk_in, uv_in,
    gqn, gqr, gl, gr, guk, guv,
    qn, qr, og, rope, uk, uv, skv, sq, kv, qd, lats,
    rm, kt, qm, qct, doct, s_all, dp_all, stats, dqt,
    dkv, rc, sy, ry, rf, sfr, rfr, rx, sdq, rdq, wsum, gp, gc, sgy, rgy, sgx, rgx, sl, rl, ag,
    load_sem, s_kvx, s_kvy, s_kvc, r_kv, s_q, r_q, s_lat, r_lat,
    s_c, r_c, s_y, r_y, s_f, r_f, s_fr, r_fr, s_x, r_x, s_dq, r_dq, s_g, r_g, s_gx, r_gx, s_l, r_l, s_a, r_a,
):
    me = lax.axis_index("ctx")
    head = lax.axis_index("head")
    x, quarter, y, core, y_mate, core_mate = place_of(me)
    z = lax.rem(head, 4)
    piece = TOKENS // heads

    def at_x(o):
        return lax.rem(x + o, 4)

    loads = [
        pltpu.make_async_copy(src, dst, load_sem.at[n])
        for n, (src, dst) in enumerate(
            (
                *((lat_in.at[:, pl.ds(128 * k, 128)], lats.at[k, x]) for k in range(4)),
                (uk_in, uk), (uv_in, uv), (rope_in, rope), (qn_in, qn), (qr_in, qr), (og_in, og),
            )
        )
    ]
    for copy in loads:
        copy.start()

    barrier = pltpu.get_barrier_semaphore()
    for o in (1, 2, 3):
        pl.semaphore_signal(
            barrier, inc=1, device_id={"ctx": 4 * at_x(o) + quarter}, device_id_type=MESH
        )
    for mate in (y_mate, core_mate):
        pl.semaphore_signal(barrier, inc=1, device_id={"ctx": mate}, device_id_type=MESH)
    for o in range(1, heads):
        pl.semaphore_signal(
            barrier, inc=1, device_id={"head": lax.rem(head + o, heads)}, device_id_type=MESH
        )

    started = []

    def send(*args):
        copy = remote(*args)
        copy.start()
        started.append(copy)

    def send_head(src, dst, send_sem, recv_sem, to):
        copy = pltpu.make_async_remote_copy(
            src_ref=src,
            dst_ref=dst,
            send_sem=send_sem,
            recv_sem=recv_sem,
            device_id={"head": to},
            device_id_type=MESH,
        )
        copy.start()
        started.append(copy)

    def wait_recv(ref, sem):
        remote(ref, ref, s_c.at[0], sem, core_mate).wait_recv()

    for copy in loads[0:7]:
        copy.wait()

    def latent_rows(block_x):
        return jnp.concatenate([lats[k, block_x] for k in range(4)], axis=1)

    latent = latent_rows(x)
    keys = jnp.dot(latent, uk[...], preferred_element_type=F32).astype(BF16)
    values = jnp.dot(latent, uv[...], preferred_element_type=F32).astype(BF16)
    rope_t = rope[...].astype(F32)
    packed_rope = jnp.concatenate([rope_t[:, 0:128], rope_t[:, 128:256]], axis=0).T.astype(BF16)
    for h in range(4):
        skv[h, 0:256, :] = keys[:, 128 * h : 128 * h + 128]
        skv[h, 256:384, :] = packed_rope
        skv[h, 384:640, :] = values[:, 128 * h : 128 * h + 128]
    pl.semaphore_wait(barrier, 5 + heads - 1)

    parts = (pl.ds(0, 384), pl.ds(384, 256))

    def send_block(ref, block, sem, n, ctx):
        for m, rows in enumerate(parts):
            send(
                ref.at[rows], kv.at[block, rows], sem.at[2 * n + m], r_kv.at[2 * block + m], ctx
            )

    def wait_block(block):
        for m, rows in enumerate(parts):
            wait_recv(kv.at[block, rows], r_kv.at[2 * block + m])

    def send_kv(o):
        send_block(skv.at[at_x(o)], me, s_kvx, o - 1, 4 * at_x(o) + quarter)

    def send_q(o):
        send(sq.at[at_x(o)], qd.at[x], s_q.at[o - 1], r_q.at[x], 4 * at_x(o) + quarter)

    send_kv(1)
    send_kv(3)
    send_block(skv.at[x], me, s_kvy, 0, y_mate)
    send_block(skv.at[x], me, s_kvc, 0, core_mate)
    low = low_lanes(128)
    for copy in loads[7:10]:
        copy.wait()
    for h in range(4):
        sq[h, 0:256, :] = qn[:, 128 * h : 128 * h + 128]
        sq[h, 256:512, :] = og[:, 128 * h : 128 * h + 128]
        tile = qr[:, 128 * (h // 2) : 128 * (h // 2) + 128].astype(F32)
        top, bottom = tile[0:128], tile[128:256]
        if h % 2 == 0:
            packed = jnp.where(low, top, swap_halves(bottom))
        else:
            packed = jnp.where(low, swap_halves(top), bottom)
        sq[h, 512:640, :] = packed.astype(BF16)
    send_q(1)
    send_q(3)
    send_kv(2)
    send_q(2)
    kv[me] = skv[x]
    qd[x] = sq[x]

    lane = lax.broadcasted_iota(jnp.int32, (128, 128), 1)

    def prepare_keys(block):
        packed = kv[block, 256:384, :].astype(F32)
        for half in range(2):
            place = order[2 * block + half]
            hidden = jnp.where(lane < 64 + place, NEG_LARGE, 0.0)
            hidden = jnp.where(lane < 96, hidden, 0.0)
            rows = packed if half == 0 else swap_halves(packed)
            rm[block, 128 * half : 128 * half + 128, :] = jnp.where(low, rows, hidden).astype(BF16)
        kt[block, 0:128, :] = kv[block, 0:256, :].T
        kt[block, 128:256, :] = rm[block].T

    def prepare_queries(slot):
        packed = qd[slot, 512:640, :].astype(F32)
        for half in range(2):
            place = order[2 * (4 * slot + quarter) + half]
            chosen = jnp.where(lane == 64 + place, 1.0, 0.0)
            rows = packed if half == 0 else swap_halves(packed)
            qm[slot, 128 * half : 128 * half + 128, :] = jnp.where(low, rows, chosen).astype(BF16)
        qct[slot, 0:128, :] = qd[slot, 0:256, :].T
        qct[slot, 128:256, :] = qm[slot].T
        doct[slot] = qd[slot, 256:512, :].T

    def scores(key_x, side, query_x, diagonal=False):
        slot = 2 * key_x + side
        pair = [4 * key_x + 2 * side + core, 4 * key_x + 2 * side + (1 - core)]
        raw, grown = [], []
        for n, block in enumerate(pair):
            keys_in = jnp.concatenate([kv[block, 0:256, :], rm[block]], axis=1)
            score = jnp.dot(keys_in, qct[query_x], preferred_element_type=F32)
            if n == 0 and diagonal:
                rows = lax.broadcasted_iota(jnp.int32, (256, 256), 0)
                columns = lax.broadcasted_iota(jnp.int32, (256, 256), 1)
                limit = jnp.where(key_x == query_x, 0, 1024)
                same = (rows < 128) == (columns < 128)
                score = jnp.where(same & (rows > columns + limit), NEG_LARGE, score)
            raw.append(score)
            dp = jnp.dot(kv[block, 384:640, :], doct[query_x], preferred_element_type=F32)
            dp_all[query_x, block] = dp
            grown.append(dp)
        tops = [jnp.max(score.reshape(32, 8, 256), axis=0) for score in raw]
        top = jnp.max(jnp.maximum(tops[0], tops[1]), axis=0, keepdims=True) * EXP2_SCALE
        total = jnp.zeros((8, 256), F32)
        weighted = jnp.zeros((8, 256), F32)
        for block, score, dp in zip(pair, raw, grown):
            p = jnp.exp2(score * EXP2_SCALE - top)
            s_all[query_x, block] = p
            total = total + jnp.sum(p.reshape(32, 8, 256), axis=0)
            weighted = weighted + jnp.sum((p * dp).reshape(32, 8, 256), axis=0)
        stats[0, query_x, slot] = top
        stats[1, query_x, slot] = jnp.sum(total, axis=0, keepdims=True)
        stats[2, query_x, slot] = jnp.sum(weighted, axis=0, keepdims=True)

    def take_x(o, n):
        block = 4 * at_x(o) + quarter
        for m, rows in enumerate(parts):
            wait_recv(kv.at[block, rows], r_kv.at[2 * block + m])
            for sem, mate in ((s_kvy, y_mate), (s_kvc, core_mate)):
                send(
                    kv.at[block, rows], kv.at[block, rows], sem.at[2 * n + m],
                    r_kv.at[2 * block + m], mate,
                )

    def take_y(o, n):
        block = 4 * at_x(o) + 2 * (1 - y) + core
        wait_block(block)
        send_block(kv.at[block], block, s_kvc, n, core_mate)

    def take_core(o, side):
        block = 4 * at_x(o) + 2 * side + (1 - core)
        wait_block(block)
        prepare_keys(4 * at_x(o) + 2 * side + core)
        prepare_keys(block)

    def take_queries(o):
        wait_recv(qd.at[at_x(o)], r_q.at[at_x(o)])
        prepare_queries(at_x(o))

    far = 1 - y
    prepare_queries(x)
    take_core(0, y)
    scores(x, y, x, True)
    take_x(1, 1)
    take_x(3, 2)
    take_y(0, 4)
    take_core(1, y)
    scores(at_x(1), y, x)
    take_core(3, y)
    scores(at_x(3), y, x)
    take_core(0, far)
    scores(x, far, x)
    take_queries(1)
    take_queries(3)

    for n in range(2):
        for o in (0, 1, 3):
            scores(at_x(o), y, at_x(1 + 2 * n), True)

    take_y(1, 5)
    take_x(2, 3)

    for n in range(2):
        scores(x, far, at_x(1 + 2 * n))

    take_core(1, far)

    for n in range(3):
        scores(at_x(1), far, at_x(n + n // 2))

    take_core(2, y)

    for n in range(3):
        scores(at_x(2), y, at_x(n + n // 2))

    take_y(3, 6)
    take_queries(2)
    for o in (1, 3, 2):
        send(lats.at[z, x], lats.at[z, x], s_lat.at[o - 1], r_lat.at[4 * z + x], 4 * at_x(o) + quarter)
    for o in range(4):
        scores(at_x(o), y, at_x(2), o == 2)
    take_core(3, far)

    for n in range(2):
        scores(at_x(3), far, at_x(2 * n))
        scores(at_x(3), far, at_x(2 * n + 1))

    take_y(2, 7)
    scores(x, far, at_x(2))
    scores(at_x(1), far, at_x(2))
    take_core(2, far)

    for n in range(2):
        scores(at_x(2), far, at_x(2 * n))
        scores(at_x(2), far, at_x(2 * n + 1))

    for n, o in enumerate((1, 3, 2)):
        other = at_x(o)
        wait_recv(lats.at[z, other], r_lat.at[4 * z + other])
        for m, oz in enumerate((1, 3, 2)):
            to = 4 * lax.div(head, 4) + lax.rem(z + oz, 4)
            send_head(
                lats.at[z, other], lats.at[z, other], s_lat.at[3 + 3 * n + m],
                r_lat.at[4 * z + other], to,
            )

    for i in range(4):
        top = stats[0, i, 0]
        for slot in range(1, 8):
            top = jnp.maximum(top, stats[0, i, slot])
        total = jnp.zeros((1, 256), F32)
        weighted = jnp.zeros((1, 256), F32)
        for slot in range(8):
            factor = jnp.exp2(stats[0, i, slot] - top)
            stats[0, i, slot] = factor
            total = total + stats[1, i, slot] * factor
            weighted = weighted + stats[2, i, slot] * factor
        inverse = 1.0 / total
        for slot in range(8):
            stats[0, i, slot] = stats[0, i, slot] * inverse
        stats[1, i, 0] = weighted * inverse
        dqt[i] = jnp.zeros((256, 256), F32)
    wsum[...] = jnp.zeros((512, 256), F32)

    def grads(slot, first, second):
        blocks = (first, second)
        dk = [jnp.zeros((256, 256), F32)] * 2
        dv = [jnp.zeros((256, 128), F32)] * 2
        for i in range(4):
            inverse, delta = stats[0, i, slot], stats[1, i, 0]
            queries = jnp.concatenate([qd[i, 0:256, :], qm[i]], axis=1)
            ds = []
            for n, block in enumerate(blocks):
                attn = s_all[i, block] * inverse
                ds.append((attn * (dp_all[i, block] - delta)).astype(BF16))
                dv[n] = dv[n] + jnp.dot(
                    attn.astype(BF16), qd[i, 256:512, :], preferred_element_type=F32
                )
                dk[n] = dk[n] + jnp.dot(ds[n], queries, preferred_element_type=F32)
            keys_t = jnp.concatenate([kt[first], kt[second]], axis=1)
            dqt[i] += jnp.dot(keys_t, jnp.concatenate(ds, axis=0), preferred_element_type=F32)
        for n, block in enumerate(blocks):
            scaled = dk[n] * SCALE
            dkv[block, 0:256, :] = scaled[:, 0:128].astype(BF16)
            dkv[block, 256:512, :] = dv[n].astype(BF16)
            tail = scaled[:, 128:256]
            dkv[block, 512:640, :] = jnp.where(low, tail[0:128], swap_halves(tail[128:256])).astype(
                BF16
            )

    def to_core(slot, block):
        return remote(dkv.at[block], rc.at[slot], s_c.at[slot], r_c.at[slot], core_mate)

    turned_rows = pl.ds(512, 128)

    def to_y(other):
        return remote(
            sy.at[other, pl.ds(0, 512)], ry.at[other], s_y.at[other], r_y.at[other], y_mate
        )

    def to_far_x(n, other):
        return remote(
            sy.at[other, turned_rows], rf.at[x], s_f.at[n], r_f.at[x], 4 * other + quarter
        )

    def pass_far(n, other):
        wait_recv(rc.at[other], r_c.at[other])
        mine = dkv[4 * other + 2 * far + core].astype(F32)
        sy[other] = (mine + rc[other].astype(F32)).astype(BF16)
        to_y(other).start()

        @pl.when(n < 3)
        def _():
            to_far_x(n, other).start()

    def whole_block(other):
        wait_recv(rc.at[4 + other], r_c.at[4 + other])
        block = 4 * other + 2 * y + core
        near = dkv[block].astype(F32) + rc[4 + other].astype(F32)
        wait_recv(ry.at[other], r_y.at[other])
        dkv[block, 0:512, :] = (near[0:512] + ry[other].astype(F32)).astype(BF16)
        dkv[block, 512:640, :] = near[512:640].astype(BF16)
        return block

    def weight_term(other):
        block = 4 * other + 2 * y + core
        pair = jnp.concatenate([dkv[block, 0:256, :], dkv[block, 256:512, :]], axis=1)
        wsum[...] += lax.dot_general(latent_rows(other), pair, TN, preferred_element_type=F32)

    def to_x(n, other, block):
        return remote(dkv.at[block], rx.at[x], s_x.at[n], r_x.at[x], 4 * other + quarter)

    def give_block(n):
        other = at_x(n + 1)
        block = whole_block(other)
        to_x(n, other, block).start()

    @pl.loop(0, 4)
    def _(n):
        other = at_x(1 + n)
        grads(2 * other + far, 4 * other + 2 * far + (1 - core), 4 * other + 2 * far + core)
        to_core(other, 4 * other + 2 * far + (1 - core)).start()
        grads(2 * other + y, 4 * other + 2 * y + (1 - core), 4 * other + 2 * y + core)
        to_core(4 + other, 4 * other + 2 * y + (1 - core)).start()
        pass_far(n, other)

        @pl.when(n > 0)
        def _():
            give_block(n - 1)

    far_turned = sy[x, 512:640, :].astype(F32)
    for o in (3, 2, 1):
        wait_recv(rf.at[at_x(o)], r_f.at[at_x(o)])
        far_turned = far_turned + rf[at_x(o)].astype(F32)
    sfr[...] = far_turned.astype(BF16)
    send(sfr, rfr, s_fr.at[0], r_fr.at[0], y_mate)
    for i in range(4):
        whole = dqt[i].T * SCALE
        sdq[i, 0:256, :] = whole[:, 0:128].astype(BF16)
        tail = whole[:, 128:256]
        sdq[i, 256:384, :] = jnp.where(low, tail[0:128], swap_halves(tail[128:256])).astype(BF16)
    rdq[x] = sdq[x]
    for o in (1, 3, 2):
        send(sdq.at[at_x(o)], rdq.at[x], s_dq.at[o - 1], r_dq.at[x], 4 * at_x(o) + quarter)

    def latent_term(h):
        columns = pl.ds(pl.multiple_of(128 * h, 128), 128)
        term = lax.dot_general(rx[h, 0:256, :], uk[:, columns], NT, preferred_element_type=F32)
        return term + lax.dot_general(
            rx[h, 256:512, :], uv[:, columns], NT, preferred_element_type=F32
        )

    summed = jnp.zeros((256, 512), F32)
    turned = jnp.zeros((128, 128), F32)
    for o in (3, 2, 0, 1):
        if o:
            wait_recv(rx.at[at_x(o)], r_x.at[at_x(o)])
        else:
            rx[x] = dkv[whole_block(x)]
        summed = summed + latent_term(at_x(o))
        turned = turned + rx[at_x(o), 512:640, :].astype(F32)
    wait_recv(rfr, r_fr.at[0])
    turned = turned + rfr[...].astype(F32)
    half = piece // 2
    for p in range(heads):
        sl[p, :, 0:512] = summed[piece * p : piece * p + piece].astype(BF16)
        sl[p, 0:half, 512:640] = turned[half * p : half * p + half].astype(BF16)
        sl[p, half:piece, 512:640] = jnp.zeros((piece - half, 128), BF16)

    for o in range(1, heads):
        to = lax.rem(head + o, heads)
        send_head(sl.at[to], rl.at[head], s_l.at[o], r_l.at[head], to)
    rl[head] = sl[head]

    for o in (1, 2, 3, 0):
        if o:
            for oz in (1, 2, 3):
                part = lax.rem(z + oz, 4)
                wait_recv(lats.at[part, at_x(o)], r_lat.at[4 * part + at_x(o)])
        weight_term(at_x(o))
    total = wsum[...].astype(BF16)
    for cc in range(2):
        for yy in range(2):
            for xx in range(4):
                row = 32 * (4 * xx + 2 * yy + cc)
                gp[cc, yy, xx] = total[row : row + 32]
    send(gp.at[1 - core], gc, s_g.at[0], r_g.at[0], core_mate)

    wait_recv(gc, r_g.at[0])
    sgy[...] = (gp[core, 1 - y].astype(F32) + gc[1 - y].astype(F32)).astype(BF16)
    send(sgy, rgy, s_g.at[1], r_g.at[1], y_mate)
    near_g = gp[core, y].astype(F32) + gc[y].astype(F32)

    for o in (1, 2, 3):
        wait_recv(rdq.at[at_x(o)], r_dq.at[at_x(o)])
    for h in range(4):
        gqn[:, 128 * h : 128 * h + 128] = rdq[h, 0:256, :]
    for two in range(2):
        a = rdq[2 * two, 256:384, :].astype(F32)
        b = rdq[2 * two + 1, 256:384, :].astype(F32)
        cols = slice(128 * two, 128 * two + 128)
        gqr[0:128, cols] = jnp.where(low, a, swap_halves(b)).astype(BF16)
        gqr[128:256, cols] = jnp.where(low, swap_halves(a), b).astype(BF16)

    wait_recv(rgy, r_g.at[1])
    sgx[...] = (near_g + rgy[...].astype(F32)).astype(BF16)
    for o in (1, 3, 2):
        send(sgx.at[at_x(o)], rgx.at[x], s_gx.at[o - 1], r_gx.at[x], 4 * at_x(o) + quarter)
    rgx[x] = sgx[x]

    for o in range(1, heads):
        source = lax.rem(head + o, heads)
        wait_recv(rl.at[source], r_l.at[source])
    over_heads = rl[0].astype(F32)
    for p in range(1, heads):
        over_heads = over_heads + rl[p].astype(F32)
    ag[head] = over_heads.astype(BF16)
    for o in range(1, heads):
        to = lax.rem(head + o, heads)
        send_head(ag.at[head], ag.at[head], s_a.at[o], r_a.at[head], to)

    for o in (1, 2, 3):
        wait_recv(rgx.at[at_x(o)], r_gx.at[at_x(o)])
    for h in range(4):
        guk[:, 128 * h : 128 * h + 128] = rgx[h, :, 0:128].astype(F32)
        guv[:, 128 * h : 128 * h + 128] = rgx[h, :, 128:256].astype(F32)

    for o in range(1, heads):
        source = lax.rem(head + o, heads)
        wait_recv(ag.at[source], r_a.at[source])
    packed = []
    for p in range(heads):
        gl[piece * p : piece * p + piece, :] = ag[p, :, 0:512].astype(F32)
        packed.append(ag[p, 0:half, 512:640].astype(F32))
    turned_t = jnp.concatenate(packed, axis=0).T
    gr[:, 0:128] = turned_t[0:64]
    gr[:, 128:256] = turned_t[64:128]

    for copy in started:
        copy.wait_send()
    for other in range(4):
        to_core(other, other).wait_send()
        to_core(4 + other, other).wait_send()
    for n in range(4):
        to_y(n).wait_send()
    for n in range(3):
        to_x(n, at_x(n + 1), 0).wait_send()
        to_far_x(n, at_x(n + 1)).wait_send()


def fused(heads, order, qn, qr, og, lat, rope_t, uk, uv):
    hbm = pl.BlockSpec(memory_space=pltpu.HBM)
    vmem = pl.BlockSpec(memory_space=pltpu.VMEM)
    piece = TOKENS // heads
    dma = pltpu.SemaphoreType.DMA
    bf = lambda *shape: pltpu.VMEM(shape, BF16)
    f32 = lambda *shape: pltpu.VMEM(shape, F32)
    return pl.pallas_call(
        functools.partial(fused_kernel, heads),
        name="fused",
        out_shape=(
            jax.ShapeDtypeStruct((TOKENS, 512), BF16),
            jax.ShapeDtypeStruct((TOKENS, 256), BF16),
            jax.ShapeDtypeStruct((TOKENS, 512), F32),
            jax.ShapeDtypeStruct((64, TOKENS), F32),
            jax.ShapeDtypeStruct((32, 512), F32),
            jax.ShapeDtypeStruct((32, 512), F32),
        ),
        in_specs=[pl.BlockSpec(memory_space=pltpu.SMEM)] + [hbm] * 7,
        out_specs=(vmem,) * 6,
        scratch_shapes=[
            bf(256, 512), bf(256, 256), bf(256, 512), bf(64, 256), bf(512, 512), bf(512, 512),
            bf(4, ROWS, 128), bf(4, ROWS, 128), bf(BLOCKS, ROWS, 128), bf(4, ROWS, 128),
            bf(4, 4, 256, 128),
            bf(BLOCKS, 256, 128), bf(BLOCKS, 256, 256), bf(4, 256, 128), bf(4, 256, 256),
            bf(4, 128, 256),
            f32(4, BLOCKS, 256, 256), f32(4, BLOCKS, 256, 256), f32(3, 4, 8, 1, 256),
            f32(4, 256, 256),
            bf(BLOCKS, ROWS, 128), bf(8, ROWS, 128), bf(4, ROWS, 128), bf(4, 512, 128),
            bf(4, 128, 128), bf(128, 128), bf(128, 128), bf(4, ROWS, 128), bf(4, DQ_ROWS, 128), bf(4, DQ_ROWS, 128),
            f32(512, 256),
            bf(2, 2, 4, 32, 256), bf(2, 4, 32, 256), bf(4, 32, 256), bf(4, 32, 256),
            bf(4, 32, 256), bf(4, 32, 256),
            bf(heads, piece, 640), bf(heads, piece, 640), bf(heads, piece, 640),
            dma((10,)), dma((6,)), dma((8,)), dma((16,)), dma((2 * BLOCKS,)), dma((3,)), dma((4,)),
            dma((12,)), dma((16,)),
            dma((8,)), dma((8,)), dma((4,)), dma((4,)), dma((4,)), dma((4,)), dma((1,)), dma((1,)),
            dma((3,)), dma((4,)), dma((3,)), dma((4,)),
            dma((2,)), dma((2,)), dma((3,)), dma((4,)),
            dma((heads,)), dma((heads,)), dma((heads,)), dma((heads,)),
        ],
        compiler_params=pltpu.CompilerParams(
            collective_id=0, has_side_effects=True, vmem_limit_bytes=60 * MIB
        ),
    )(order, qn, qr, og, lat, rope_t, uk, uv)


def finish_kernel(*refs):
    sources, results, sems = refs[0:6], refs[6:12], refs[12]
    copies = [
        pltpu.make_async_copy(src, dst, sems.at[n]) for n, (src, dst) in enumerate(zip(sources, results))
    ]
    for copy in copies:
        copy.start()
    for copy in copies:
        copy.wait()


def finish(*arrays):
    vmem = pl.BlockSpec(memory_space=pltpu.VMEM)
    hbm = pl.BlockSpec(memory_space=pltpu.HBM)
    return pl.pallas_call(
        finish_kernel,
        name="finish",
        out_shape=tuple(jax.ShapeDtypeStruct(a.shape, a.dtype) for a in arrays),
        in_specs=[vmem] * 6,
        out_specs=(hbm,) * 6,
        scratch_shapes=[pltpu.SemaphoreType.DMA((6,))],
    )(*arrays)


def per_device(q_nope, q_rope, latent, rope_keys, out_grad, up_keys, up_values, group_order):
    outs = fused(
        lax.axis_size("head"), group_order, q_nope, q_rope, out_grad, latent, rope_keys.T,
        up_keys, up_values,
    )
    outs = finish(*outs)
    return (outs[0], outs[1], outs[2], outs[3].T, outs[4], outs[5])


def solution(mesh):
    in_specs = (
        P("ctx", "head"),
        P("ctx", "head"),
        P("ctx", None),
        P("ctx", None),
        P("ctx", "head"),
        P(None, "head"),
        P(None, "head"),
        P(),
    )
    out_specs = (
        P("ctx", "head"),
        P("ctx", "head"),
        P("ctx", None),
        P("ctx", None),
        P("ctx", "head"),
        P("ctx", "head"),
    )
    return jax.shard_map(
        per_device, mesh=mesh, in_specs=in_specs, out_specs=out_specs, check_vma=False
    )
```

```python
import functools
import math

import jax
import jax.numpy as jnp
from jax import lax
from jax.experimental import pallas as pl
from jax.experimental.pallas import tpu as pltpu
from jax.sharding import PartitionSpec as P

MESH = pl.DeviceIdType.MESH
F32 = jnp.float32
BF16 = jnp.bfloat16

SCALE = (128 + 64) ** (-0.5)
EXP2_SCALE = SCALE * math.log2(math.e)
NEG_LARGE = -1e30

GROUP = 128
GROUPS = 32
BLOCKS = 16
TOKENS = 256
ROWS = 640
DQ_ROWS = 384
MIB = 1024 * 1024

NT = (((1,), (1,)), ((), ()))
TN = (((0,), (0,)), ((), ()))


def low_lanes(rows):
    return lax.broadcasted_iota(jnp.int32, (rows, 128), 1) < 64


def swap_halves(tile):
    return pltpu.roll(tile, 64, 1)


def place_of(me):
    x = lax.div(me, 4)
    quarter = lax.rem(me, 4)
    core = lax.rem(quarter, 2)
    y = lax.div(quarter, 2)
    y_mate = 4 * x + 2 * (1 - y) + core
    core_mate = 4 * x + 2 * y + (1 - core)
    return x, quarter, y, core, y_mate, core_mate


def remote(src, dst, send_sem, recv_sem, ctx):
    return pltpu.make_async_remote_copy(
        src_ref=src,
        dst_ref=dst,
        send_sem=send_sem,
        recv_sem=recv_sem,
        device_id={"ctx": ctx},
        device_id_type=MESH,
    )


def fused_kernel(
    heads, order, qn_in, qr_in, og_in, lat_in, rope_in, uk_in, uv_in,
    gqn, gqr, gl, gr, guk, guv,
    qn, qr, og, rope, uk, uv, skv, sq, kv, qd, lats,
    rm, kt, qm, qct, doct, s_all, dp_all, stats, dqt,
    dkv, rc, sy, ry, rf, sfr, rfr, rx, sdq, rdq, wsum, gp, gc, sgy, rgy, sgx, rgx, sl, rl, ag,
    load_sem, s_kvx, s_kvy, s_kvc, r_kv, s_q, r_q, s_lat, r_lat,
    s_c, r_c, s_y, r_y, s_f, r_f, s_fr, r_fr, s_x, r_x, s_dq, r_dq, s_g, r_g, s_gx, r_gx, s_l, r_l, s_a, r_a,
):
    me = lax.axis_index("ctx")
    head = lax.axis_index("head")
    x, quarter, y, core, y_mate, core_mate = place_of(me)
    z = lax.rem(head, 4)
    piece = TOKENS // heads

    def at_x(o):
        return lax.rem(x + o, 4)

    loads = [
        pltpu.make_async_copy(src, dst, load_sem.at[n])
        for n, (src, dst) in enumerate(
            (
                *((lat_in.at[:, pl.ds(128 * k, 128)], lats.at[k, x]) for k in range(4)),
                (uk_in, uk), (uv_in, uv), (rope_in, rope), (qn_in, qn), (qr_in, qr), (og_in, og),
            )
        )
    ]
    for copy in loads:
        copy.start()

    barrier = pltpu.get_barrier_semaphore()
    for o in (1, 2, 3):
        pl.semaphore_signal(
            barrier, inc=1, device_id={"ctx": 4 * at_x(o) + quarter}, device_id_type=MESH
        )
    for mate in (y_mate, core_mate):
        pl.semaphore_signal(barrier, inc=1, device_id={"ctx": mate}, device_id_type=MESH)
    for o in range(1, heads):
        pl.semaphore_signal(
            barrier, inc=1, device_id={"head": lax.rem(head + o, heads)}, device_id_type=MESH
        )

    far_first = (6, 5, 7, 4, 2, 1, 3)

    def head_peer(o):
        return 4 * lax.rem(lax.div(head, 4) + o // 4, 2) + lax.rem(z + o % 4, 4)

    started = []

    def send(*args):
        copy = remote(*args)
        copy.start()
        started.append(copy)

    def send_head(src, dst, send_sem, recv_sem, to):
        copy = pltpu.make_async_remote_copy(
            src_ref=src,
            dst_ref=dst,
            send_sem=send_sem,
            recv_sem=recv_sem,
            device_id={"head": to},
            device_id_type=MESH,
        )
        copy.start()
        started.append(copy)

    def wait_recv(ref, sem):
        remote(ref, ref, s_c.at[0], sem, core_mate).wait_recv()

    for copy in loads[0:7]:
        copy.wait()

    def latent_rows(block_x):
        return jnp.concatenate([lats[k, block_x] for k in range(4)], axis=1)

    latent = latent_rows(x)
    keys = jnp.dot(latent, uk[...], preferred_element_type=F32).astype(BF16)
    values = jnp.dot(latent, uv[...], preferred_element_type=F32).astype(BF16)
    rope_t = rope[...].astype(F32)
    packed_rope = jnp.concatenate([rope_t[:, 0:128], rope_t[:, 128:256]], axis=0).T.astype(BF16)
    for h in range(4):
        skv[h, 0:256, :] = keys[:, 128 * h : 128 * h + 128]
        skv[h, 256:384, :] = packed_rope
        skv[h, 384:640, :] = values[:, 128 * h : 128 * h + 128]
    pl.semaphore_wait(barrier, 5 + heads - 1)

    parts = (pl.ds(0, 384), pl.ds(384, 256))

    def send_block(ref, block, sem, n, ctx):
        for m, rows in enumerate(parts):
            send(
                ref.at[rows], kv.at[block, rows], sem.at[2 * n + m], r_kv.at[2 * block + m], ctx
            )

    def wait_block(block):
        for m, rows in enumerate(parts):
            wait_recv(kv.at[block, rows], r_kv.at[2 * block + m])

    def send_kv(o):
        send_block(skv.at[at_x(o)], me, s_kvx, o - 1, 4 * at_x(o) + quarter)

    def send_q(o):
        send(sq.at[at_x(o)], qd.at[x], s_q.at[o - 1], r_q.at[x], 4 * at_x(o) + quarter)

    send_kv(1)
    send_kv(3)
    send_block(skv.at[x], me, s_kvy, 0, y_mate)
    send_block(skv.at[x], me, s_kvc, 0, core_mate)
    low = low_lanes(128)
    for copy in loads[7:10]:
        copy.wait()
    for h in range(4):
        sq[h, 0:256, :] = qn[:, 128 * h : 128 * h + 128]
        sq[h, 256:512, :] = og[:, 128 * h : 128 * h + 128]
        tile = qr[:, 128 * (h // 2) : 128 * (h // 2) + 128].astype(F32)
        top, bottom = tile[0:128], tile[128:256]
        if h % 2 == 0:
            packed = jnp.where(low, top, swap_halves(bottom))
        else:
            packed = jnp.where(low, swap_halves(top), bottom)
        sq[h, 512:640, :] = packed.astype(BF16)
    send_q(1)
    send_q(3)
    send_kv(2)
    send_q(2)
    kv[me] = skv[x]
    qd[x] = sq[x]

    lane = lax.broadcasted_iota(jnp.int32, (128, 128), 1)

    def prepare_keys(block):
        packed = kv[block, 256:384, :].astype(F32)
        for half in range(2):
            place = order[2 * block + half]
            hidden = jnp.where(lane < 64 + place, NEG_LARGE, 0.0)
            hidden = jnp.where(lane < 96, hidden, 0.0)
            rows = packed if half == 0 else swap_halves(packed)
            rm[block, 128 * half : 128 * half + 128, :] = jnp.where(low, rows, hidden).astype(BF16)
        kt[block, 0:128, :] = kv[block, 0:256, :].T
        kt[block, 128:256, :] = rm[block].T

    def prepare_queries(slot):
        packed = qd[slot, 512:640, :].astype(F32)
        for half in range(2):
            place = order[2 * (4 * slot + quarter) + half]
            chosen = jnp.where(lane == 64 + place, 1.0, 0.0)
            rows = packed if half == 0 else swap_halves(packed)
            qm[slot, 128 * half : 128 * half + 128, :] = jnp.where(low, rows, chosen).astype(BF16)
        qct[slot, 0:128, :] = qd[slot, 0:256, :].T
        qct[slot, 128:256, :] = qm[slot].T
        doct[slot] = qd[slot, 256:512, :].T

    def scores(key_x, side, query_x, diagonal=False):
        slot = 2 * key_x + side
        pair = [4 * key_x + 2 * side + core, 4 * key_x + 2 * side + (1 - core)]
        raw, grown = [], []
        for n, block in enumerate(pair):
            keys_in = jnp.concatenate([kv[block, 0:256, :], rm[block]], axis=1)
            score = jnp.dot(keys_in, qct[query_x], preferred_element_type=F32)
            if n == 0 and diagonal:
                rows = lax.broadcasted_iota(jnp.int32, (256, 256), 0)
                columns = lax.broadcasted_iota(jnp.int32, (256, 256), 1)
                limit = jnp.where(key_x == query_x, 0, 1024)
                same = (rows < 128) == (columns < 128)
                score = jnp.where(same & (rows > columns + limit), NEG_LARGE, score)
            raw.append(score)
            dp = jnp.dot(kv[block, 384:640, :], doct[query_x], preferred_element_type=F32)
            dp_all[query_x, block] = dp
            grown.append(dp)
        tops = [jnp.max(score.reshape(32, 8, 256), axis=0) for score in raw]
        top = jnp.max(jnp.maximum(tops[0], tops[1]), axis=0, keepdims=True) * EXP2_SCALE
        total = jnp.zeros((8, 256), F32)
        weighted = jnp.zeros((8, 256), F32)
        for block, score, dp in zip(pair, raw, grown):
            p = jnp.exp2(score * EXP2_SCALE - top)
            s_all[query_x, block] = p
            total = total + jnp.sum(p.reshape(32, 8, 256), axis=0)
            weighted = weighted + jnp.sum((p * dp).reshape(32, 8, 256), axis=0)
        stats[0, query_x, slot] = top
        stats[1, query_x, slot] = jnp.sum(total, axis=0, keepdims=True)
        stats[2, query_x, slot] = jnp.sum(weighted, axis=0, keepdims=True)

    def take_x(o, n):
        block = 4 * at_x(o) + quarter
        for m, rows in enumerate(parts):
            wait_recv(kv.at[block, rows], r_kv.at[2 * block + m])
            for sem, mate in ((s_kvy, y_mate), (s_kvc, core_mate)):
                send(
                    kv.at[block, rows], kv.at[block, rows], sem.at[2 * n + m],
                    r_kv.at[2 * block + m], mate,
                )

    def take_y(o, n):
        block = 4 * at_x(o) + 2 * (1 - y) + core
        wait_block(block)
        send_block(kv.at[block], block, s_kvc, n, core_mate)

    def take_core(o, side):
        block = 4 * at_x(o) + 2 * side + (1 - core)
        wait_block(block)
        prepare_keys(4 * at_x(o) + 2 * side + core)
        prepare_keys(block)

    def take_queries(o):
        wait_recv(qd.at[at_x(o)], r_q.at[at_x(o)])
        prepare_queries(at_x(o))

    far = 1 - y
    prepare_queries(x)
    take_core(0, y)
    scores(x, y, x, True)
    take_x(1, 1)
    take_x(3, 2)
    take_y(0, 4)
    take_core(1, y)
    scores(at_x(1), y, x)
    take_core(3, y)
    scores(at_x(3), y, x)
    take_core(0, far)
    scores(x, far, x)
    take_queries(1)
    take_queries(3)

    for n in range(2):
        for o in (0, 1, 3):
            scores(at_x(o), y, at_x(1 + 2 * n), True)

    take_y(1, 5)
    take_x(2, 3)

    for n in range(2):
        scores(x, far, at_x(1 + 2 * n))

    take_core(1, far)

    for n in range(3):
        scores(at_x(1), far, at_x(n + n // 2))

    take_core(2, y)

    for n in range(3):
        scores(at_x(2), y, at_x(n + n // 2))

    take_y(3, 6)
    take_queries(2)
    for o in (1, 3, 2):
        send(lats.at[z, x], lats.at[z, x], s_lat.at[o - 1], r_lat.at[4 * z + x], 4 * at_x(o) + quarter)
    for o in range(4):
        scores(at_x(o), y, at_x(2), o == 2)
    take_core(3, far)

    for n in range(2):
        scores(at_x(3), far, at_x(2 * n))
        scores(at_x(3), far, at_x(2 * n + 1))

    take_y(2, 7)
    scores(x, far, at_x(2))
    scores(at_x(1), far, at_x(2))
    take_core(2, far)

    for n in range(2):
        scores(at_x(2), far, at_x(2 * n))
        scores(at_x(2), far, at_x(2 * n + 1))

    for n, o in enumerate((1, 3, 2)):
        other = at_x(o)
        wait_recv(lats.at[z, other], r_lat.at[4 * z + other])
        for m, oz in enumerate((1, 3, 2)):
            to = 4 * lax.div(head, 4) + lax.rem(z + oz, 4)
            send_head(
                lats.at[z, other], lats.at[z, other], s_lat.at[3 + 3 * n + m],
                r_lat.at[4 * z + other], to,
            )

    for i in range(4):
        top = stats[0, i, 0]
        for slot in range(1, 8):
            top = jnp.maximum(top, stats[0, i, slot])
        total = jnp.zeros((1, 256), F32)
        weighted = jnp.zeros((1, 256), F32)
        for slot in range(8):
            factor = jnp.exp2(stats[0, i, slot] - top)
            stats[0, i, slot] = factor
            total = total + stats[1, i, slot] * factor
            weighted = weighted + stats[2, i, slot] * factor
        inverse = 1.0 / total
        for slot in range(8):
            stats[0, i, slot] = stats[0, i, slot] * inverse
        stats[1, i, 0] = weighted * inverse
        dqt[i] = jnp.zeros((256, 256), F32)
    wsum[...] = jnp.zeros((512, 256), F32)

    def grads(slot, first, second):
        blocks = (first, second)
        dk = [jnp.zeros((256, 256), F32)] * 2
        dv = [jnp.zeros((256, 128), F32)] * 2
        for i in range(4):
            inverse, delta = stats[0, i, slot], stats[1, i, 0]
            queries = jnp.concatenate([qd[i, 0:256, :], qm[i]], axis=1)
            ds = []
            for n, block in enumerate(blocks):
                attn = s_all[i, block] * inverse
                ds.append((attn * (dp_all[i, block] - delta)).astype(BF16))
                dv[n] = dv[n] + jnp.dot(
                    attn.astype(BF16), qd[i, 256:512, :], preferred_element_type=F32
                )
                dk[n] = dk[n] + jnp.dot(ds[n], queries, preferred_element_type=F32)
            keys_t = jnp.concatenate([kt[first], kt[second]], axis=1)
            dqt[i] += jnp.dot(keys_t, jnp.concatenate(ds, axis=0), preferred_element_type=F32)
        for n, block in enumerate(blocks):
            scaled = dk[n] * SCALE
            dkv[block, 0:256, :] = scaled[:, 0:128].astype(BF16)
            dkv[block, 256:512, :] = dv[n].astype(BF16)
            tail = scaled[:, 128:256]
            dkv[block, 512:640, :] = jnp.where(low, tail[0:128], swap_halves(tail[128:256])).astype(
                BF16
            )

    def to_core(slot, block):
        return remote(dkv.at[block], rc.at[slot], s_c.at[slot], r_c.at[slot], core_mate)

    turned_rows = pl.ds(512, 128)

    def to_y(other):
        return remote(
            sy.at[other, pl.ds(0, 512)], ry.at[other], s_y.at[other], r_y.at[other], y_mate
        )

    def to_far_x(n, other):
        return remote(
            sy.at[other, turned_rows], rf.at[x], s_f.at[n], r_f.at[x], 4 * other + quarter
        )

    def pass_far(n, other):
        wait_recv(rc.at[other], r_c.at[other])
        mine = dkv[4 * other + 2 * far + core].astype(F32)
        sy[other] = (mine + rc[other].astype(F32)).astype(BF16)
        to_y(other).start()

        if n < 3:
            to_far_x(n, other).start()

    def whole_block(other):
        wait_recv(rc.at[4 + other], r_c.at[4 + other])
        block = 4 * other + 2 * y + core
        near = dkv[block].astype(F32) + rc[4 + other].astype(F32)
        wait_recv(ry.at[other], r_y.at[other])
        dkv[block, 0:512, :] = (near[0:512] + ry[other].astype(F32)).astype(BF16)
        dkv[block, 512:640, :] = near[512:640].astype(BF16)
        return block

    def weight_term(other):
        block = 4 * other + 2 * y + core
        pair = jnp.concatenate([dkv[block, 0:256, :], dkv[block, 256:512, :]], axis=1)
        wsum[...] += lax.dot_general(latent_rows(other), pair, TN, preferred_element_type=F32)

    def to_x(n, other, block):
        return remote(dkv.at[block], rx.at[x], s_x.at[n], r_x.at[x], 4 * other + quarter)

    def give_block(n):
        other = at_x(n + 1)
        block = whole_block(other)
        to_x(n, other, block).start()

    for n in range(4):
        other = at_x(1 + n)
        grads(2 * other + far, 4 * other + 2 * far + (1 - core), 4 * other + 2 * far + core)
        to_core(other, 4 * other + 2 * far + (1 - core)).start()
        grads(2 * other + y, 4 * other + 2 * y + (1 - core), 4 * other + 2 * y + core)
        to_core(4 + other, 4 * other + 2 * y + (1 - core)).start()
        pass_far(n, other)

        if n > 0:
            give_block(n - 1)

    far_turned = sy[x, 512:640, :].astype(F32)
    for o in (3, 2, 1):
        wait_recv(rf.at[at_x(o)], r_f.at[at_x(o)])
        far_turned = far_turned + rf[at_x(o)].astype(F32)
    sfr[...] = far_turned.astype(BF16)
    send(sfr, rfr, s_fr.at[0], r_fr.at[0], y_mate)
    for i in range(4):
        whole = dqt[i].T * SCALE
        sdq[i, 0:256, :] = whole[:, 0:128].astype(BF16)
        tail = whole[:, 128:256]
        sdq[i, 256:384, :] = jnp.where(low, tail[0:128], swap_halves(tail[128:256])).astype(BF16)
    rdq[x] = sdq[x]

    def latent_term(h):
        columns = pl.ds(pl.multiple_of(128 * h, 128), 128)
        term = lax.dot_general(rx[h, 0:256, :], uk[:, columns], NT, preferred_element_type=F32)
        return term + lax.dot_general(
            rx[h, 256:512, :], uv[:, columns], NT, preferred_element_type=F32
        )

    summed = jnp.zeros((256, 512), F32)
    turned = jnp.zeros((128, 128), F32)
    for o in (3, 2, 0, 1):
        if o:
            wait_recv(rx.at[at_x(o)], r_x.at[at_x(o)])
        else:
            rx[x] = dkv[whole_block(x)]
        summed = summed + latent_term(at_x(o))
        turned = turned + rx[at_x(o), 512:640, :].astype(F32)
    wait_recv(rfr, r_fr.at[0])
    turned = turned + rfr[...].astype(F32)
    half = piece // 2
    for p in range(heads):
        sl[p, :, 0:512] = summed[piece * p : piece * p + piece].astype(BF16)
        sl[p, 0:half, 512:640] = turned[half * p : half * p + half].astype(BF16)
        sl[p, half:piece, 512:640] = jnp.zeros((piece - half, 128), BF16)

    for o in far_first:
        to = head_peer(o)
        send_head(sl.at[to], rl.at[head], s_l.at[o], r_l.at[head], to)
    for o in (1, 3, 2):
        send(sdq.at[at_x(o)], rdq.at[x], s_dq.at[o - 1], r_dq.at[x], 4 * at_x(o) + quarter)
    rl[head] = sl[head]

    for o in (1, 2, 3, 0):
        if o:
            for oz in (1, 2, 3):
                part = lax.rem(z + oz, 4)
                wait_recv(lats.at[part, at_x(o)], r_lat.at[4 * part + at_x(o)])
        weight_term(at_x(o))
    total = wsum[...].astype(BF16)
    for cc in range(2):
        for yy in range(2):
            for xx in range(4):
                row = 32 * (4 * xx + 2 * yy + cc)
                gp[cc, yy, xx] = total[row : row + 32]
    send(gp.at[1 - core], gc, s_g.at[0], r_g.at[0], core_mate)

    wait_recv(gc, r_g.at[0])
    sgy[...] = (gp[core, 1 - y].astype(F32) + gc[1 - y].astype(F32)).astype(BF16)
    send(sgy, rgy, s_g.at[1], r_g.at[1], y_mate)
    near_g = gp[core, y].astype(F32) + gc[y].astype(F32)

    for o in range(1, heads):
        source = lax.rem(head + o, heads)
        wait_recv(rl.at[source], r_l.at[source])
    over_heads = rl[0].astype(F32)
    for p in range(1, heads):
        over_heads = over_heads + rl[p].astype(F32)
    ag[head] = over_heads.astype(BF16)
    for o in far_first:
        to = head_peer(o)
        send_head(ag.at[head], ag.at[head], s_a.at[o], r_a.at[head], to)

    for o in (1, 2, 3):
        wait_recv(rdq.at[at_x(o)], r_dq.at[at_x(o)])
    for h in range(4):
        gqn[:, 128 * h : 128 * h + 128] = rdq[h, 0:256, :]
    for two in range(2):
        a = rdq[2 * two, 256:384, :].astype(F32)
        b = rdq[2 * two + 1, 256:384, :].astype(F32)
        cols = slice(128 * two, 128 * two + 128)
        gqr[0:128, cols] = jnp.where(low, a, swap_halves(b)).astype(BF16)
        gqr[128:256, cols] = jnp.where(low, swap_halves(a), b).astype(BF16)

    wait_recv(rgy, r_g.at[1])
    sgx[...] = (near_g + rgy[...].astype(F32)).astype(BF16)
    for o in (1, 3, 2):
        send(sgx.at[at_x(o)], rgx.at[x], s_gx.at[o - 1], r_gx.at[x], 4 * at_x(o) + quarter)
    rgx[x] = sgx[x]

    for o in (1, 2, 3):
        wait_recv(rgx.at[at_x(o)], r_gx.at[at_x(o)])
    for h in range(4):
        guk[:, 128 * h : 128 * h + 128] = rgx[h, :, 0:128].astype(F32)
        guv[:, 128 * h : 128 * h + 128] = rgx[h, :, 128:256].astype(F32)

    for o in range(1, heads):
        source = lax.rem(head + o, heads)
        wait_recv(ag.at[source], r_a.at[source])
    packed = []
    for p in range(heads):
        gl[piece * p : piece * p + piece, :] = ag[p, :, 0:512].astype(F32)
        packed.append(ag[p, 0:half, 512:640].astype(F32))
    turned_t = jnp.concatenate(packed, axis=0).T
    gr[:, 0:128] = turned_t[0:64]
    gr[:, 128:256] = turned_t[64:128]

    for copy in started:
        copy.wait_send()
    for other in range(4):
        to_core(other, other).wait_send()
        to_core(4 + other, other).wait_send()
    for n in range(4):
        to_y(n).wait_send()
    for n in range(3):
        to_x(n, at_x(n + 1), 0).wait_send()
        to_far_x(n, at_x(n + 1)).wait_send()


def fused(heads, order, qn, qr, og, lat, rope_t, uk, uv):
    hbm = pl.BlockSpec(memory_space=pltpu.HBM)
    vmem = pl.BlockSpec(memory_space=pltpu.VMEM)
    piece = TOKENS // heads
    dma = pltpu.SemaphoreType.DMA
    bf = lambda *shape: pltpu.VMEM(shape, BF16)
    f32 = lambda *shape: pltpu.VMEM(shape, F32)
    return pl.pallas_call(
        functools.partial(fused_kernel, heads),
        name="fused",
        out_shape=(
            jax.ShapeDtypeStruct((TOKENS, 512), BF16),
            jax.ShapeDtypeStruct((TOKENS, 256), BF16),
            jax.ShapeDtypeStruct((TOKENS, 512), F32),
            jax.ShapeDtypeStruct((64, TOKENS), F32),
            jax.ShapeDtypeStruct((32, 512), F32),
            jax.ShapeDtypeStruct((32, 512), F32),
        ),
        in_specs=[pl.BlockSpec(memory_space=pltpu.SMEM)] + [hbm] * 7,
        out_specs=(vmem,) * 6,
        scratch_shapes=[
            bf(256, 512), bf(256, 256), bf(256, 512), bf(64, 256), bf(512, 512), bf(512, 512),
            bf(4, ROWS, 128), bf(4, ROWS, 128), bf(BLOCKS, ROWS, 128), bf(4, ROWS, 128),
            bf(4, 4, 256, 128),
            bf(BLOCKS, 256, 128), bf(BLOCKS, 256, 256), bf(4, 256, 128), bf(4, 256, 256),
            bf(4, 128, 256),
            f32(4, BLOCKS, 256, 256), f32(4, BLOCKS, 256, 256), f32(3, 4, 8, 1, 256),
            f32(4, 256, 256),
            bf(BLOCKS, ROWS, 128), bf(8, ROWS, 128), bf(4, ROWS, 128), bf(4, 512, 128),
            bf(4, 128, 128), bf(128, 128), bf(128, 128), bf(4, ROWS, 128), bf(4, DQ_ROWS, 128), bf(4, DQ_ROWS, 128),
            f32(512, 256),
            bf(2, 2, 4, 32, 256), bf(2, 4, 32, 256), bf(4, 32, 256), bf(4, 32, 256),
            bf(4, 32, 256), bf(4, 32, 256),
            bf(heads, piece, 640), bf(heads, piece, 640), bf(heads, piece, 640),
            dma((10,)), dma((6,)), dma((8,)), dma((16,)), dma((2 * BLOCKS,)), dma((3,)), dma((4,)),
            dma((12,)), dma((16,)),
            dma((8,)), dma((8,)), dma((4,)), dma((4,)), dma((4,)), dma((4,)), dma((1,)), dma((1,)),
            dma((3,)), dma((4,)), dma((3,)), dma((4,)),
            dma((2,)), dma((2,)), dma((3,)), dma((4,)),
            dma((heads,)), dma((heads,)), dma((heads,)), dma((heads,)),
        ],
        compiler_params=pltpu.CompilerParams(
            collective_id=0, has_side_effects=True, vmem_limit_bytes=60 * MIB
        ),
    )(order, qn, qr, og, lat, rope_t, uk, uv)


def finish_kernel(*refs):
    sources, results, sems = refs[0:6], refs[6:12], refs[12]
    copies = [
        pltpu.make_async_copy(src, dst, sems.at[n]) for n, (src, dst) in enumerate(zip(sources, results))
    ]
    for copy in copies:
        copy.start()
    for copy in copies:
        copy.wait()


def finish(*arrays):
    vmem = pl.BlockSpec(memory_space=pltpu.VMEM)
    hbm = pl.BlockSpec(memory_space=pltpu.HBM)
    return pl.pallas_call(
        finish_kernel,
        name="finish",
        out_shape=tuple(jax.ShapeDtypeStruct(a.shape, a.dtype) for a in arrays),
        in_specs=[vmem] * 6,
        out_specs=(hbm,) * 6,
        scratch_shapes=[pltpu.SemaphoreType.DMA((6,))],
    )(*arrays)


def per_device(q_nope, q_rope, latent, rope_keys, out_grad, up_keys, up_values, group_order):
    outs = fused(
        lax.axis_size("head"), group_order, q_nope, q_rope, out_grad, latent, rope_keys.T,
        up_keys, up_values,
    )
    outs = finish(*outs)
    return (outs[0], outs[1], outs[2], outs[3].T, outs[4], outs[5])


def solution(mesh):
    in_specs = (
        P("ctx", "head"),
        P("ctx", "head"),
        P("ctx", None),
        P("ctx", None),
        P("ctx", "head"),
        P(None, "head"),
        P(None, "head"),
        P(),
    )
    out_specs = (
        P("ctx", "head"),
        P("ctx", "head"),
        P("ctx", None),
        P("ctx", None),
        P("ctx", "head"),
        P("ctx", "head"),
    )
    return jax.shard_map(
        per_device, mesh=mesh, in_specs=in_specs, out_specs=out_specs, check_vma=False
    )
```
